32 devices in a mesh: tile: 8 (over z, y), row: 2 (over core), col: 2 (over x).
Axes of the slice: x: 2, y: 2, z: 4, core: 2. Of those that a mesh axis runs over, the one named last changes fastest.
Arguments:
- tile_tokens: bfloat16 [96, 256, 1536], P(('tile', 'row', 'col')), may hold values from -6 to 6
- tile_count: int32 [32], replicated, may hold values from 1 to 3, as said below
- tile_cell: int32 [96], replicated, may hold values from 0 to 127, as said below
- occupancy: int32 [32, 4], replicated, may hold values from 0 to 1, as said below
- block_mask: int32 [16, 2, 8], P(('tile', 'row'), 'col'), may hold values 0 or 1
- enc_gain: float32 [1536], replicated, may hold values from 0.25 to 1.75
- w_query: bfloat16 [1536, 768], P('tile'), may hold values from -1 to 1
- w_key: bfloat16 [1536, 768], P('tile'), may hold values from -1 to 1
- w_value: bfloat16 [1536, 768], P('tile'), may hold values from -0.15625 to 0.15625
- w_out_t: bfloat16 [1536, 768], P('tile'), may hold values from -0.21875 to 0.21875
- final_gain: float32 [1536], replicated, may hold values from 0.25 to 1.75
- w_proj: bfloat16 [1536, 768], P('tile'), may hold values from -0.15625 to 0.15625
- slide_gain: float32 [768], replicated, may hold values from 0.25 to 1.75
- s_query: bfloat16 [768, 384], P('tile'), may hold values from -1 to 1
- s_key: bfloat16 [768, 384], P('tile'), may hold values from -1 to 1
- s_value: bfloat16 [768, 384], P('tile'), may hold values from -0.21875 to 0.21875
- s_out_t: bfloat16 [768, 384], P('tile'), may hold values from -0.3125 to 0.3125
Outputs:
- grid_tokens: bfloat16 [32, 4, 768], P(('tile', 'row'), 'col')
- slide_branch: float32 [32, 4, 768], P(('tile', 'row'), 'col')
The draws below stay inside these ranges and needn't reach their ends.
Inputs may be any that keep to these rules, and one draw needn't show every extreme that they name: Only the first tile_count[d] slots of device d hold tissue tiles; some device holds exactly 3. `tile_cell`: A slot of the device with indices (t, r, c) lies in grid column block c and in a grid row block b * 2 + r for some b, blocks being 2 x 2 cells. No two slots share a cell. The slots of one device lie in distinct row blocks, and for each slot number the slots of the 8 devices (t, r, c) with fixed r and c lie in distinct row blocks. `occupancy`: 1 exactly at the cells of the live slots.
All inputs are finite; a program needn't handle non-finite values. No bound on the sum of `block_mask` on one device may be relied on, other than what follows from the above.
Results may differ from the reference program's by a relative error of at most 0.017.
Values may be sent and summed in bfloat16 or wider, within the bound.
A program may use at most 64 MiB of HBM per device.

```python
import math
import jax
import jax.numpy as jnp
from jax import lax

E = 1536
HT = 12
HD = 64
PATCH = 256
D = 768
HS = 8
HDS = 48
BLOCK = 2
TILE_DEV = 3
TILES = 96
GRID_ROWS = 32
GRID_COLS = 4
N_TILE = 8
N_ROW = 2
N_COL = 2


def tissue_layout(key):
    count_key, pick_key, owner_key, seat_key = jax.random.split(key, 4)
    devices_all = N_TILE * N_ROW * N_COL
    groups = N_ROW * N_COL
    counts = jax.random.randint(count_key, (devices_all,), 1, TILE_DEV + 1)
    chosen = jax.random.randint(pick_key, (), 0, devices_all)
    counts = jnp.where(jnp.arange(devices_all) == chosen, TILE_DEV, counts).astype(jnp.int32)
    orders = jax.vmap(lambda each_key: jax.random.permutation(each_key, N_TILE))(jax.random.split(owner_key, groups))
    seat_order = jax.vmap(lambda each_key: jax.random.permutation(each_key, BLOCK * BLOCK))(jax.random.split(seat_key, groups * N_TILE)).reshape(groups, N_TILE, BLOCK * BLOCK)
    stride = N_TILE // TILE_DEV
    slot_ids = jnp.arange(TILE_DEV)
    owners = (orders[:, :, None] + slot_ids[None, None, :] * stride) % N_TILE
    group_ids = jnp.arange(groups)[:, None, None]
    local_cell = seat_order[group_ids, owners, slot_ids[None, None, :]]
    row_index = group_ids // N_COL
    column_index = group_ids % N_COL
    grid_row = (owners * N_ROW + row_index) * BLOCK + local_cell // BLOCK
    grid_col = column_index * BLOCK + local_cell % BLOCK
    cell_index = grid_row * GRID_COLS + grid_col
    cell_index = cell_index.reshape(N_ROW, N_COL, N_TILE, TILE_DEV).transpose(2, 0, 1, 3).reshape(-1).astype(jnp.int32)
    live_slot = (slot_ids[None, :] < counts[:, None]).reshape(-1).astype(jnp.int32)
    occupied = jnp.zeros((GRID_ROWS * GRID_COLS,), jnp.int32).at[cell_index].max(live_slot).reshape(GRID_ROWS, GRID_COLS)
    return (counts, cell_index, occupied)


def draw_tile_count(key, part):
    return tissue_layout(key)[0]


def draw_tile_cell(key, part):
    return tissue_layout(key)[1]


def draw_occupancy(key, part):
    return tissue_layout(key)[2]


def draw_tile_tokens(key, part):
    key = jax.random.fold_in(key, 11)
    base_key = jax.random.fold_in(key, 0)
    shape = (TILES, PATCH, E)
    tokens = jax.random.normal(base_key, shape, jnp.float32)
    tokens = tokens.at[:, 0, :].multiply(0.25)
    return jnp.clip(tokens, -6.0, 6.0).astype(jnp.bfloat16)


def draw_w_query(key, part):
    key = jax.random.fold_in(key, 21)
    own_noise = jax.random.normal(key, (E, HT * HD), jnp.float32)
    return jnp.clip(own_noise / E ** 0.5, -1.0, 1.0).astype(jnp.bfloat16)


def draw_w_key(key, part):
    key = jax.random.fold_in(key, 22)
    own_noise = jax.random.normal(key, (E, HT * HD), jnp.float32)
    return jnp.clip(own_noise / E ** 0.5, -1.0, 1.0).astype(jnp.bfloat16)


def draw_s_query(key, part):
    key = jax.random.fold_in(key, 31)
    own_noise = jax.random.normal(key, (D, HS * HDS), jnp.float32)
    return jnp.clip(own_noise / D ** 0.5, -1.0, 1.0).astype(jnp.bfloat16)


def draw_s_key(key, part):
    key = jax.random.fold_in(key, 32)
    own_noise = jax.random.normal(key, (D, HS * HDS), jnp.float32)
    return jnp.clip(own_noise / D ** 0.5, -1.0, 1.0).astype(jnp.bfloat16)


def plant(result, rng, low, high):
    extent = result.shape
    index_at = [jax.random.randint(jax.random.fold_in(rng, axis), (), 0, extent[axis]) for axis in range(len(extent))]
    result = result.at[tuple(index_at)].set(low)
    longest = extent.index(max(extent))
    index_at[longest] = (index_at[longest] + 1) % extent[longest]
    return result.at[tuple(index_at)].set(high)


def block_scale(own_key, extent, shards, smallest, top_value):
    loudness, own = 1.0, jax.random.fold_in(own_key, 6)
    for position, shards_of in shards:
        steps = jnp.exp(jax.random.uniform(jax.random.fold_in(own, position), (shards_of,), jnp.float32, smallest / len(shards), top_value / len(shards)))
        loudness = loudness * jnp.repeat(steps, extent[position] // shards_of).reshape([-1 if axis == position else 1 for axis in range(len(extent))])
    return loudness


def scatter_about(own_key, extent, deviation, most, shards=(), dtype=jnp.bfloat16):
    drawn = deviation * jax.random.normal(own_key, extent, jnp.float32)
    if shards:
        drawn = drawn * block_scale(own_key, extent, shards, -0.22, 0.18)
    return jnp.clip(drawn, -most, most).astype(dtype)


def setup_inputs(seed: int = 0) -> dict:
    key_list = jax.random.split(jax.random.key(seed), 18)
    tile_tokens = draw_tile_tokens(jax.random.fold_in(key_list[17], 71), 0)
    tile_count = draw_tile_count(jax.random.fold_in(key_list[17], 71), 0)
    tile_cell = draw_tile_cell(jax.random.fold_in(key_list[17], 71), 0)
    occupancy = draw_occupancy(jax.random.fold_in(key_list[17], 71), 0)
    block_mask = plant((jax.random.randint(key_list[4], (GRID_ROWS // BLOCK, GRID_COLS // BLOCK, 8), 0, 4) < 3).astype(jnp.int32), jax.random.fold_in(key_list[4], 1), 0, 1)
    enc_gain = jnp.clip(1.0 + 0.15 * jax.random.normal(key_list[5], (E,), jnp.float32), 0.25, 1.75)
    w_query = draw_w_query(jax.random.fold_in(key_list[17], 71), 0)
    w_key = draw_w_key(jax.random.fold_in(key_list[17], 71), 0)
    w_value = scatter_about(key_list[8], (E, HT * HD), E ** -0.5, 0.15625, ((0, 8),))
    w_out_t = scatter_about(key_list[9], (E, HT * HD), (HT * HD) ** -0.5, 0.21875, ((0, 8),))
    final_gain = jnp.clip(1.0 + 0.15 * jax.random.normal(key_list[10], (E,), jnp.float32), 0.25, 1.75)
    w_proj = scatter_about(key_list[11], (E, D), E ** -0.5, 0.15625, ((0, 8),))
    slide_gain = jnp.clip(1.0 + 0.15 * jax.random.normal(key_list[12], (D,), jnp.float32), 0.25, 1.75)
    s_query = draw_s_query(jax.random.fold_in(key_list[17], 71), 0)
    s_key = draw_s_key(jax.random.fold_in(key_list[17], 71), 0)
    s_value = scatter_about(key_list[15], (D, HS * HDS), D ** -0.5, 0.21875, ((0, 8),))
    s_out_t = scatter_about(key_list[16], (D, HS * HDS), (HS * HDS) ** -0.5, 0.3125, ((0, 8),))
    return {"tile_tokens": tile_tokens, "tile_count": tile_count, "tile_cell": tile_cell, "occupancy": occupancy, "block_mask": block_mask, "enc_gain": enc_gain, "w_query": w_query, "w_key": w_key, "w_value": w_value, "w_out_t": w_out_t, "final_gain": final_gain, "w_proj": w_proj, "slide_gain": slide_gain, "s_query": s_query, "s_key": s_key, "s_value": s_value, "s_out_t": s_out_t}


def layer_norm(vector, scale_gain, epsilon):
    row_mean = lax.optimization_barrier(jnp.mean(vector, axis=-1, keepdims=True))
    centered = vector - row_mean
    spread = lax.optimization_barrier(jnp.mean(centered * centered, axis=-1, keepdims=True))
    return centered * lax.rsqrt(spread + epsilon) * scale_gain

def rounded(vector):
    return lax.optimization_barrier(vector.astype(jnp.bfloat16)).astype(jnp.float32)

def encode_tile(one_tile, weights):
    enc_gain, query_full, key_full, value_full, out_full, final_gain, w_proj = weights
    highest = lax.Precision.HIGHEST
    wide_tile = one_tile.astype(jnp.float32)
    normed = rounded(layer_norm(wide_tile, enc_gain, 1e-06))
    class_query = rounded(jnp.dot(normed[0:1], query_full, precision=highest))
    tile_keys = rounded(jnp.dot(normed, key_full, precision=highest))
    tile_values = rounded(jnp.dot(normed, value_full, precision=highest))
    head_count = class_query.shape[1] // HD
    scores = jnp.einsum('hd,phd->hp', class_query.reshape(head_count, HD), tile_keys.reshape(-1, head_count, HD), precision=highest) / math.sqrt(HD)
    row_peak = lax.optimization_barrier(jnp.max(scores, axis=1, keepdims=True))
    weights_exp = jnp.exp(scores - row_peak)
    soft = rounded(weights_exp / lax.optimization_barrier(jnp.sum(weights_exp, axis=1, keepdims=True)))
    class_mix = rounded(jnp.einsum('hp,phd->hd', soft, tile_values.reshape(-1, head_count, HD), precision=highest).reshape(1, -1))
    carried = wide_tile[0:1] + lax.dot_general(class_mix, out_full, (((1,), (1,)), ((), ())), precision=highest)
    final_rows = layer_norm(carried, final_gain, 1e-06).astype(jnp.bfloat16)
    return jnp.dot(final_rows, w_proj, preferred_element_type=jnp.float32).astype(jnp.bfloat16)[0]

def reference(tile_tokens, tile_count, tile_cell, occupancy, block_mask, enc_gain, w_query, w_key, w_value, w_out_t, final_gain, w_proj, slide_gain, s_query, s_key, s_value, s_out_t):
    highest = lax.Precision.HIGHEST
    weights = (enc_gain, w_query.astype(jnp.float32), w_key.astype(jnp.float32), w_value.astype(jnp.float32), w_out_t.astype(jnp.float32), final_gain, w_proj)
    embedded = lax.map(lambda one_tile: encode_tile(one_tile, weights), tile_tokens)
    slot_live = (jnp.arange(TILE_DEV)[None, :] < tile_count[:, None]).reshape(-1)
    placed = jnp.where(slot_live[:, None], embedded.astype(jnp.float32), jnp.zeros((), jnp.float32))
    grid_flat = jnp.zeros((GRID_ROWS * GRID_COLS, D), jnp.float32).at[tile_cell.astype(jnp.int32)].add(placed)
    grid_tokens = grid_flat.astype(jnp.bfloat16).reshape(GRID_ROWS, GRID_COLS, D)
    slide_in = rounded(layer_norm(grid_tokens.astype(jnp.float32), slide_gain, 1e-05))

    def project(matrix):
        return rounded(jnp.einsum('rcd,de->rce', slide_in, matrix.astype(jnp.float32), precision=highest))
    slide_query = project(s_query)
    slide_keys = project(s_key)
    slide_values = project(s_value)
    block_rows = GRID_ROWS // BLOCK
    block_cols = GRID_COLS // BLOCK

    def blocked(field):
        return field.reshape(block_rows, BLOCK, block_cols, BLOCK, -1).transpose(0, 2, 1, 3, 4).reshape(block_rows, block_cols, BLOCK * BLOCK, -1)

    def beside_all(field):
        padded = jnp.pad(field, ((1, 1), (1, 1), (0, 0), (0, 0)))
        return jnp.concatenate([padded[1 + row_step:1 + row_step + block_rows, 1 + col_step:1 + col_step + block_cols] for row_step in (-1, 0, 1) for col_step in (-1, 0, 1)], axis=2)
    near_keys = beside_all(blocked(slide_keys))
    near_values = beside_all(blocked(slide_values))
    live_cells = blocked(occupancy[:, :, None].astype(jnp.float32))
    near_live = beside_all(live_cells)[..., 0]
    mask_full = jnp.concatenate([block_mask[:, :, :4], jnp.ones_like(block_mask[:, :, :1]), block_mask[:, :, 4:]], axis=2).astype(jnp.float32)
    usable = near_live * jnp.repeat(mask_full, BLOCK * BLOCK, axis=2) > 0
    head_count = slide_query.shape[-1] // HDS
    query_heads = blocked(slide_query).reshape(block_rows, block_cols, BLOCK * BLOCK, head_count, HDS)
    key_heads = near_keys.reshape(block_rows, block_cols, -1, head_count, HDS)
    value_heads = near_values.reshape(block_rows, block_cols, -1, head_count, HDS)
    scores = jnp.einsum('abqhd,abkhd->abhqk', query_heads, key_heads, precision=highest) / math.sqrt(HDS)
    allow = usable[:, :, None, None, :]
    row_peak = lax.optimization_barrier(jnp.max(jnp.where(allow, scores, -1e+30), axis=-1, keepdims=True))
    weights_exp = jnp.where(allow, jnp.exp(scores - row_peak), jnp.zeros((), jnp.float32))
    query_live = live_cells[:, :, None, :, :]
    soft = rounded(weights_exp / (lax.optimization_barrier(jnp.sum(weights_exp, axis=-1, keepdims=True)) + 1.0 - query_live) * query_live)
    slide_mix = rounded(jnp.einsum('abhqk,abkhd->abqhd', soft, value_heads, precision=highest).reshape(block_rows, block_cols, BLOCK * BLOCK, -1))
    branch = jnp.einsum('abqs,ds->abqd', slide_mix, s_out_t.astype(jnp.float32), precision=highest)
    branch = branch.reshape(block_rows, block_cols, BLOCK, BLOCK, D).transpose(0, 2, 1, 3, 4).reshape(GRID_ROWS, GRID_COLS, D)
    return (grid_tokens, branch)
```

```python
import math

import jax
import jax.numpy as jnp
from jax import lax
from jax.experimental import pallas as pl
from jax.experimental.pallas import tpu as pltpu
from jax.sharding import PartitionSpec as P

HD = 64
HDS = 48
BLOCK = 2


def with_halo(cells, sides, width):
    for axis, dim in sides:
        count = lax.axis_size(axis)
        ends = count - 1
        head = lax.slice_in_dim(cells, 0, width, axis=dim)
        tail = lax.slice_in_dim(cells, cells.shape[dim] - width, cells.shape[dim], axis=dim)
        cells = jnp.concatenate(
            [
                lax.ppermute(tail, axis, [(i, (i + 1) % count) for i in range(ends)]),
                cells,
                lax.ppermute(head, axis, [((i + 1) % count, i) for i in range(ends)]),
            ],
            axis=dim,
        )
    return cells


def layer_norm(vector, scale_gain, epsilon):
    row_mean = jnp.mean(vector, axis=-1, keepdims=True)
    centered = vector - row_mean
    spread = jnp.mean(centered * centered, axis=-1, keepdims=True)
    return centered * lax.rsqrt(spread + epsilon) * scale_gain


def contract_last(first_op, second_op):
    return lax.dot_general(
        first_op,
        second_op,
        (((first_op.ndim - 1,), (1,)), ((), ())),
        preferred_element_type=jnp.float32,
    )


def class_branch(one_tile, query_row, enc_gain, key_part, value_part):
    wide_tile = one_tile.astype(jnp.float32)
    normed = layer_norm(wide_tile, enc_gain, 1e-06).astype(jnp.bfloat16)
    tile_keys = jnp.dot(normed, key_part, preferred_element_type=jnp.float32).astype(jnp.bfloat16)
    tile_values = jnp.dot(normed, value_part, preferred_element_type=jnp.float32).astype(
        jnp.bfloat16
    )
    head_count = key_part.shape[1] // HD
    scores = jnp.einsum(
        "hd,phd->hp",
        query_row.reshape(head_count, HD),
        tile_keys.reshape(-1, head_count, HD),
        preferred_element_type=jnp.float32,
    ) / math.sqrt(HD)
    row_peak = jnp.max(scores, axis=1, keepdims=True)
    weights_exp = jnp.exp(scores - row_peak)
    soft = (weights_exp / jnp.sum(weights_exp, axis=1, keepdims=True)).astype(jnp.bfloat16)
    return (
        jnp.einsum(
            "hp,phd->hd",
            soft,
            tile_values.reshape(-1, head_count, HD),
            preferred_element_type=jnp.float32,
        )
        .reshape(1, -1)
        .astype(jnp.bfloat16)
    )


def partial_rows(buffer, queries, low_row, high_row, weights, out_part):
    enc_gain, key_part, value_part = weights
    row_width = out_part.shape[0]

    def one_slot(slot_index, running):
        one_tile = lax.dynamic_index_in_dim(buffer, slot_index, 0, keepdims=False)
        query_row = lax.dynamic_index_in_dim(queries, slot_index, 0, keepdims=False)
        class_mix = class_branch(one_tile, query_row, enc_gain, key_part, value_part)
        result_row = contract_last(class_mix, out_part)[0]
        return lax.dynamic_update_index_in_dim(running, result_row, slot_index, 0)

    blank_rows = jnp.zeros((buffer.shape[0], row_width), jnp.float32)
    return lax.fori_loop(low_row, high_row, one_slot, blank_rows)


def encode_segment(buffer, queries, low_row, high_row, weights, out_part, final_gain, w_proj):
    partial_value = partial_rows(buffer, queries, low_row, high_row, weights, out_part)
    carried = buffer[:, 0, :].astype(jnp.float32) + partial_value
    final_rows = layer_norm(carried, final_gain, 1e-06).astype(jnp.bfloat16)
    result = jnp.dot(final_rows, w_proj, preferred_element_type=jnp.float32).astype(jnp.bfloat16)
    slot_ids = jnp.arange(buffer.shape[0])
    kept = (slot_ids >= low_row) & (slot_ids < high_row)
    return jnp.where(kept[:, None], result, jnp.zeros_like(result))


def local(
    tile_tokens,
    tile_count,
    tile_cell,
    occupancy,
    block_mask,
    enc_gain,
    w_query,
    w_key,
    w_value,
    w_out_t,
    final_gain,
    w_proj,
    slide_gain,
    s_query,
    s_key,
    s_value,
    s_out_t,
):
    tile_devices = lax.axis_size("tile")
    row_devices = lax.axis_size("row")
    column_devices = lax.axis_size("col")
    tile_index = lax.axis_index("tile")
    row_index = lax.axis_index("row")
    column_index = lax.axis_index("col")
    slot_total = tile_tokens.shape[0]
    counts = tile_count.reshape(tile_devices, row_devices, column_devices)
    class_raw = tile_tokens[:, 0, :]
    key_value = (
        lax.all_gather(w_key, "tile", axis=0, tiled=True),
        lax.all_gather(w_value, "tile", axis=0, tiled=True),
    )
    weights = (enc_gain, key_value[0], key_value[1])
    class_side = (
        lax.all_gather(w_query, "tile", axis=0, tiled=True),
        lax.all_gather(w_out_t, "tile", axis=0, tiled=True),
        lax.all_gather(w_proj, "tile", axis=0, tiled=True),
    )
    own_normed = layer_norm(class_raw.astype(jnp.float32), enc_gain, 1e-06).astype(jnp.bfloat16)
    queries = jnp.dot(own_normed, class_side[0], preferred_element_type=jnp.float32).astype(
        jnp.bfloat16
    )
    out_part = class_side[1]
    full_proj = class_side[2]
    slide_full = (
        lax.all_gather(s_query, "tile", axis=0, tiled=True),
        lax.all_gather(s_key, "tile", axis=0, tiled=True),
        lax.all_gather(s_value, "tile", axis=0, tiled=True),
        lax.all_gather(s_out_t, "tile", axis=0, tiled=True),
    )
    own_count = counts[tile_index, row_index, column_index]
    encoded = encode_segment(
        tile_tokens, queries, 0, own_count, weights, out_part, final_gain, full_proj
    )
    width_model = encoded.shape[1]
    group_cells = tile_cell.reshape(tile_devices, row_devices, column_devices, slot_total)[
        :, row_index, column_index, :
    ]
    live_slots = jnp.arange(slot_total)[None, :] < counts[:, row_index, column_index][:, None]
    grid_cols = BLOCK * column_devices
    grid_row = group_cells // grid_cols
    grid_col = group_cells % grid_cols
    owner_tile = grid_row // BLOCK // row_devices
    local_cell = grid_row % BLOCK * BLOCK + grid_col % BLOCK
    mine_mask = live_slots & (owner_tile == tile_index)
    cell_ids = jnp.arange(BLOCK * BLOCK)
    my_owner = owner_tile[tile_index]
    my_live = live_slots[tile_index]
    selector = ((my_owner[None, :] == jnp.arange(tile_devices)[:, None]) & my_live[None, :]).astype(
        jnp.bfloat16
    )
    outgoing = jnp.dot(selector, encoded, preferred_element_type=jnp.float32).astype(jnp.bfloat16)
    incoming = lax.all_to_all(outgoing, "tile", split_axis=0, concat_axis=0, tiled=True)
    placement = jnp.any(
        (local_cell[None, :, :] == cell_ids[:, None, None]) & mine_mask[None, :, :], axis=2
    ).astype(jnp.bfloat16)
    block_cells = jnp.dot(placement, incoming, preferred_element_type=jnp.float32)
    grid_tokens = block_cells.astype(jnp.bfloat16).reshape(BLOCK, BLOCK, width_model)
    slide_in = layer_norm(block_cells, slide_gain, 1e-05).astype(jnp.bfloat16)
    slide_query = jnp.dot(slide_in, slide_full[0], preferred_element_type=jnp.float32).astype(
        jnp.bfloat16
    )
    slide_keys = jnp.dot(slide_in, slide_full[1], preferred_element_type=jnp.float32).astype(
        jnp.bfloat16
    )
    slide_values = jnp.dot(slide_in, slide_full[2], preferred_element_type=jnp.float32).astype(
        jnp.bfloat16
    )
    inner_width = slide_keys.shape[1]
    key_value_cells = jnp.concatenate([slide_keys, slide_values], axis=1).reshape(
        BLOCK, BLOCK, 2 * inner_width
    )
    surround = with_halo(key_value_cells, ((("tile", "row"), 0), ("col", 1)), BLOCK)
    near_rows = surround.reshape(-1, 2 * inner_width)
    near_keys = near_rows[:, :inner_width]
    near_values = near_rows[:, inner_width:]
    block_row = tile_index * row_devices + row_index
    padded = jnp.pad(occupancy, BLOCK)
    window = lax.dynamic_slice(
        padded, (block_row * BLOCK, column_index * BLOCK), (3 * BLOCK, 3 * BLOCK)
    )
    mask_row = block_mask.reshape(-1)
    mask_grid = jnp.concatenate([mask_row[:4], jnp.ones((1,), jnp.int32), mask_row[4:]]).reshape(
        3, 3
    )
    mask_cells = jnp.repeat(jnp.repeat(mask_grid, BLOCK, axis=0), BLOCK, axis=1)
    usable = (window * mask_cells).reshape(-1) > 0
    query_live = (
        lax.dynamic_slice(occupancy, (block_row * BLOCK, column_index * BLOCK), (BLOCK, BLOCK))
        .reshape(-1)
        .astype(jnp.float32)
    )
    head_count = inner_width // HDS
    scores = jnp.einsum(
        "qhd,khd->hqk",
        slide_query.reshape(-1, head_count, HDS),
        near_keys.reshape(-1, head_count, HDS),
        preferred_element_type=jnp.float32,
    ) / math.sqrt(HDS)
    allow = usable[None, None, :]
    row_peak = jnp.max(jnp.where(allow, scores, -1e30), axis=-1, keepdims=True)
    weights_exp = jnp.where(allow, jnp.exp(scores - row_peak), 0.0)
    live_query = query_live[None, :, None]
    soft = (
        weights_exp / (jnp.sum(weights_exp, axis=-1, keepdims=True) + 1.0 - live_query) * live_query
    ).astype(jnp.bfloat16)
    slide_mix = (
        jnp.einsum(
            "hqk,khd->qhd",
            soft,
            near_values.reshape(-1, head_count, HDS),
            preferred_element_type=jnp.float32,
        )
        .reshape(-1, inner_width)
        .astype(jnp.bfloat16)
    )
    slide_branch = contract_last(slide_mix, slide_full[3]).reshape(BLOCK, BLOCK, width_model)
    return (grid_tokens, slide_branch)


MESH_ID = pl.DeviceIdType.MESH
NEAR = [(-1, -1), (-1, 0), (-1, 1), (0, -1), (0, 1), (1, -1), (1, 0), (1, 1)]
FAR_BIAS = -1e30
PHASES = 8


def fits_fused(mesh):
    return mesh.shape["tile"] == 8 and mesh.shape["row"] == 2


def contract_rows(first_op, second_op):
    return lax.dot_general(
        first_op, second_op, (((1,), (1,)), ((), ())), preferred_element_type=jnp.float32
    )


def matmul(first_op, second_op):
    return jnp.dot(first_op, second_op, preferred_element_type=jnp.float32)


def fused_kernel(
    sizes,
    cell_ref,
    count_ref,
    mask_ref,
    tok_hbm,
    enc_gain_ref,
    final_gain_ref,
    slide_gain_ref,
    wq_ref,
    wk_ref,
    wv_ref,
    wo_ref,
    wp_ref,
    sq_ref,
    sk_ref,
    sv_ref,
    so_ref,
    grid_ref,
    branch_ref,
    cls,
    tok,
    normed,
    s1,
    r1,
    s2,
    r2,
    s3,
    r3,
    s4,
    r4,
    s5,
    r5,
    s6,
    r6,
    s7,
    r7,
    s9,
    r9,
    sg,
    rg,
    halo_out,
    halo,
    wide,
    gains,
    live,
    slide_w,
    in_sem,
    send_sem,
    recv_sem,
    w_send,
    w_recv,
    halo_send,
    halo_recv,
):
    tiles, rows_n, cols_n, slots, patch, width, inner = sizes
    shard = width // tiles
    half = inner // 2
    heads = inner // HD
    half_heads = heads // 2
    bf, f32 = jnp.bfloat16, jnp.float32
    me = lax.axis_index("tile")
    my_row = lax.axis_index("row")
    my_col = lax.axis_index("col")
    block_row = me * rows_n + my_row

    first_in = pltpu.make_async_copy(tok_hbm.at[:, pl.ds(0, 16), :], cls, in_sem.at[0])
    first_in.start()
    whole_in = pltpu.make_async_copy(tok_hbm, tok, in_sem.at[1])
    whole_in.start()

    blank = jnp.where(
        lax.broadcasted_iota(jnp.int32, (8, halo.shape[2]), 1) == halo_lane(halo), FAR_BIAS, 0.0
    )
    for place in range(9):
        halo[place] = blank

    barrier = pltpu.get_barrier_semaphore()
    for step in range(1, tiles):
        pl.semaphore_signal(
            barrier, inc=1, device_id={"tile": lax.rem(me + step, tiles)}, device_id_type=MESH_ID
        )
    beside = []
    near_count = jnp.int32(0)
    for down, right in NEAR:
        to_row = block_row + down
        to_col = my_col + right
        inside = (to_row >= 0) & (to_row < tiles * rows_n) & (to_col >= 0) & (to_col < cols_n)
        target = {
            "tile": lax.div(to_row + rows_n, rows_n) - 1,
            "row": lax.rem(to_row + rows_n, rows_n),
            "col": to_col,
        }
        beside.append((inside, target))
        near_count = near_count + inside.astype(jnp.int32)

        @pl.when(inside)
        def greet(target=target):
            pl.semaphore_signal(barrier, inc=1, device_id=target, device_id_type=MESH_ID)

    first_in.wait()
    raw = [cls[slot].astype(f32)[0:1] for slot in range(slots)]
    raw_rows = jnp.concatenate(raw, axis=0)
    enc_gain = enc_gain_ref[...]
    class_normed = layer_norm(raw_rows, enc_gain, 1e-06).astype(bf).astype(f32)
    class_rows = jnp.concatenate(
        [class_normed, raw_rows, jnp.zeros((8 - 2 * slots, width), f32)], axis=0
    )
    for to in range(tiles):
        s1[to, :, :shard] = class_rows[:, to * shard : (to + 1) * shard]
        gains[to, :, :shard] = jnp.broadcast_to(
            final_gain_ref[:, to * shard : (to + 1) * shard], (8, shard)
        )

    pl.semaphore_wait(barrier, tiles - 1 + near_count)

    started = []

    def send(phase, source, landing):
        copies = []
        for step in range(1, tiles):
            to = lax.rem(me + step, tiles)
            copy = pltpu.make_async_remote_copy(
                src_ref=source.at[to] if len(source.shape) == len(landing.shape) else source,
                dst_ref=landing.at[me],
                send_sem=send_sem.at[phase, step],
                recv_sem=recv_sem.at[phase, step],
                device_id={"tile": to},
                device_id_type=MESH_ID,
            )
            copy.start()
            copies.append(copy)
        started.extend(copies)
        landing[me] = source[me] if len(source.shape) == len(landing.shape) else source[...]
        return copies

    def arrive(copies):
        for copy in copies:
            copy.wait_recv()

    copies1 = send(0, s1, r1)

    own_pair = pl.ds(my_row * 2, 2)
    first_core = my_row == 0
    slide_w[my_row * 2, me] = jnp.where(first_core, sq_ref[...], sv_ref[...])
    slide_w[my_row * 2 + 1, me] = jnp.where(first_core, sk_ref[...], so_ref[...])
    w_copies = []
    for step in range(1, tiles):
        copy = pltpu.make_async_remote_copy(
            src_ref=slide_w.at[own_pair, me],
            dst_ref=slide_w.at[own_pair, me],
            send_sem=w_send.at[step],
            recv_sem=w_recv.at[step],
            device_id={"tile": lax.rem(me + step, tiles)},
            device_id_type=MESH_ID,
        )
        copy.start()
        w_copies.append(copy)

    row64 = lax.broadcasted_iota(jnp.int32, (8 * tiles, 1), 0)
    in_block = lax.rem(row64, 8)

    def norm_chunk(chunk, carry):
        rows = pl.ds(pl.multiple_of(chunk * 32, 32), 32)
        inside = pl.ds(pl.multiple_of(lax.rem(chunk, per_tile) * 32, 32), 32)
        wide_rows_in = tok[lax.div(chunk, per_tile), inside, :].astype(f32)
        normed[rows, :] = layer_norm(wide_rows_in, enc_gain, 1e-06).astype(bf)
        return carry

    per_tile = patch // 32
    whole_chunks = slots * per_tile
    whole_in.wait()
    my_gain = gains[me][:, :shard]
    gain_high = my_gain.astype(bf)
    gain_low = (my_gain - gain_high.astype(f32)).astype(bf)
    sums = [
        matmul(gain_high, wp_ref[:, cut : cut + half])
        + matmul(gain_low, wp_ref[:, cut : cut + half])
        for cut in (0, half)
    ]
    low_rows = lax.broadcasted_iota(jnp.int32, (8, 1), 0) < 4
    sg[...] = jnp.where(low_rows, sums[0], sums[1])
    copies_g = send(7, sg, rg)

    col64 = lax.broadcasted_iota(jnp.int32, (8 * tiles, 8 * tiles), 1)
    row_full = lax.broadcasted_iota(jnp.int32, (8 * tiles, 8 * tiles), 0)
    place_low = jnp.zeros((8 * tiles, 8 * tiles), f32)
    grid_cols = BLOCK * cols_n
    group = my_row * cols_n + my_col
    row_key = lax.div(row_full, 8) * 4 + lax.rem(row_full, 4)
    for other in range(tiles):
        device = other * rows_n * cols_n + group
        count = count_ref[device]
        for slot in range(slots):
            cell = cell_ref[device * slots + slot]
            cell_row = lax.div(cell, jnp.int32(grid_cols))
            cell_col = lax.rem(cell, jnp.int32(grid_cols))
            owner = lax.div(cell_row, jnp.int32(BLOCK * rows_n))
            spot = owner * 4 + lax.rem(cell_row, BLOCK) * BLOCK + lax.rem(cell_col, BLOCK)
            spot = jnp.where(slot < count, spot, -1)
            hit = (row_key == spot) & (col64 == other * 8 + slot)
            place_low = jnp.where(hit, 1.0, place_low)
    place_high = jnp.concatenate([jnp.zeros((8 * tiles, slots), f32), place_low[:, :-slots]], axis=1)
    live_col = jnp.sum(place_low, axis=1, keepdims=True)
    live[...] = jnp.broadcast_to(live_col, (8 * tiles, 128)).reshape(tiles, 8, 128)
    place_low = place_low.astype(bf)
    place_high = place_high.astype(bf)

    arrive(copies1)
    shards1 = r1[...].reshape(8 * tiles, r1.shape[2])[:, :shard].astype(bf)
    part_low = matmul(shards1, wq_ref[:, :half])
    part_high = matmul(shards1, wq_ref[:, half:])
    shifted = jnp.concatenate([part_high[-slots:], part_high[:-slots]], axis=0)
    s2[...] = jnp.where(in_block < slots, part_low, shifted).reshape(s2.shape)
    copies2 = send(1, s2, r2)
    lax.fori_loop(0, whole_chunks // 3, norm_chunk, 0)
    arrive(copies2)
    s3[...] = jnp.sum(r2[...], axis=0).astype(bf).astype(f32)
    copies3 = send(2, s3, r3)
    lax.fori_loop(whole_chunks // 3, 2 * (whole_chunks // 3), norm_chunk, 0)

    wide_rows = 48 * tiles
    exp_row = lax.broadcasted_iota(jnp.int32, (wide_rows, 8 * tiles), 0)
    exp_col = lax.broadcasted_iota(jnp.int32, (wide_rows, 8 * tiles), 1)
    exp_in = lax.rem(exp_row, 48)
    exp_slot = lax.div(exp_in, heads)
    exp_head = lax.rem(exp_in, heads)
    exp_base = lax.div(exp_row, 48) * 8 + exp_slot
    real = exp_slot < slots
    pick_low = (real & (exp_head < half_heads) & (exp_col == exp_base)).astype(f32).astype(bf)
    pick_high = (
        (real & (exp_head >= half_heads) & (exp_col == exp_base + slots)).astype(f32).astype(bf)
    )
    head_of_row = lax.rem(
        lax.rem(lax.broadcasted_iota(jnp.int32, (wide_rows, half), 0), 48), heads
    )
    head_of_col = lax.div(lax.broadcasted_iota(jnp.int32, (wide_rows, half), 1), HD)
    own_low = head_of_row == head_of_col
    own_high = head_of_row == head_of_col + half_heads
    arrive(copies3)
    queries = r3[...].reshape(8 * tiles, half).astype(bf)
    query_low = jnp.where(own_low, matmul(pick_low, queries), 0.0).astype(bf)
    query_high = jnp.where(own_high, matmul(pick_high, queries), 0.0).astype(bf)
    folded = contract_rows(query_low, wk_ref[:, :half]) + contract_rows(
        query_high, wk_ref[:, half:]
    )
    s4[:, :, :shard] = folded.astype(bf).reshape(tiles, 48, shard)
    copies4 = send(3, s4, r4)
    lax.fori_loop(2 * (whole_chunks // 3), whole_chunks, norm_chunk, 0)
    arrive(copies4)

    for other in range(tiles):
        wide[:, other * shard : (other + 1) * shard] = r4[other, :, :shard]
    tokens = normed[...]
    scores = contract_rows(wide[...], tokens) / math.sqrt(HD)
    score_slot = lax.div(lax.broadcasted_iota(jnp.int32, scores.shape, 0), heads)
    score_tile = lax.div(lax.broadcasted_iota(jnp.int32, scores.shape, 1), patch)
    same = score_slot == score_tile
    peak = jnp.max(jnp.where(same, scores, -1e30), axis=1, keepdims=True)
    grown = jnp.where(same, jnp.exp(jnp.minimum(scores - peak, 0.0)), 0.0)
    total = jnp.sum(grown, axis=1, keepdims=True)
    probs = (grown / jnp.where(total > 0.0, total, 1.0)).astype(bf)
    mixed = matmul(probs, tokens).astype(bf)
    for to in range(tiles):
        s5[to, :, :shard] = mixed[:, to * shard : (to + 1) * shard]
    copies5 = send(4, s5, r5)
    arrive(copies5)

    mixes = r5[...].reshape(wide_rows, r5.shape[2])[:, :shard]
    value_low = jnp.where(own_low, matmul(mixes, wv_ref[:, :half]), 0.0).astype(bf)
    value_high = jnp.where(own_high, matmul(mixes, wv_ref[:, half:]), 0.0).astype(bf)
    columns0 = (((0,), (0,)), ((), ()))
    gathered = lax.dot_general(
        pick_low, value_low, columns0, preferred_element_type=f32
    ) + lax.dot_general(pick_high, value_high, columns0, preferred_element_type=f32)
    s6[...] = gathered.reshape(s6.shape)
    copies6 = send(5, s6, r6)
    arrive(copies6)
    s7[...] = jnp.sum(r6[...], axis=0).astype(bf).astype(f32)
    copies7 = send(6, s7, r7)
    raw_cells = matmul(place_high, shards1)

    for copy in w_copies:
        copy.wait_recv()
    pair_copy = pltpu.make_async_remote_copy(
        src_ref=slide_w.at[own_pair],
        dst_ref=slide_w.at[own_pair],
        send_sem=w_send.at[0],
        recv_sem=w_recv.at[0],
        device_id={"row": 1 - my_row},
        device_id_type=MESH_ID,
    )
    pair_copy.start()
    arrive(copies7)

    mix_rows = r7[...].reshape(8 * tiles, half).astype(bf)
    cell_low = matmul(place_low, mix_rows).astype(bf)
    cell_high = matmul(place_high, mix_rows).astype(bf)
    carried = (
        raw_cells
        + contract_rows(cell_low, wo_ref[:, :half])
        + contract_rows(cell_high, wo_ref[:, half:])
    )
    part_mean = jnp.mean(carried, axis=1, keepdims=True)
    centered = carried - part_mean
    part_square = jnp.sum(centered * centered, axis=1, keepdims=True)
    scaled = (centered * my_gain[0:1]).astype(bf)
    landed = jnp.where(
        in_block < 4, matmul(scaled, wp_ref[:, :half]), matmul(scaled, wp_ref[:, half:])
    )
    s9[:, :, :half] = landed.reshape(tiles, 8, half)
    lane = lax.broadcasted_iota(jnp.int32, (8 * tiles, 128), 1)
    s9[:, :, half:] = jnp.where(lane == 0, part_mean, part_square).reshape(tiles, 8, 128)
    copies9 = send(8, s9, r9)
    arrive(copies_g)
    arrive(copies9)

    means = [r9[other, :, half : half + 1] for other in range(tiles)]
    mean = sum(means) / tiles
    square = sum(
        r9[other, :, half + 1 : half + 2] + shard * (means[other] - mean) ** 2
        for other in range(tiles)
    )
    joined = sum(
        r9[other, :, :half] + (means[other] - mean) * rg[other] for other in range(tiles)
    )
    joined = (joined * lax.rsqrt(square / width + 1e-06)).astype(bf)
    cells32 = joined.astype(f32)
    cells = jnp.concatenate([cells32[0:4], cells32[4:8]], axis=1)
    grid_ref[0] = cells[0:2].astype(bf)
    grid_ref[1] = cells[2:4].astype(bf)

    pair_copy.wait_recv()
    inner_s = so_ref.shape[1]
    slide_rows = jnp.concatenate([cells, cells], axis=0)
    slide_in = layer_norm(slide_rows, slide_gain_ref[...], 1e-05).astype(bf)

    def slide_full(which):
        return slide_w[which].reshape(-1, inner_s)

    keys = matmul(slide_in, slide_full(1))
    values = matmul(slide_in, slide_full(2))
    my_live = live[me][:, 0:1]
    halo_out[:, :inner_s] = jnp.where(low_rows, keys, values).astype(bf).astype(f32)
    lane8 = lax.broadcasted_iota(jnp.int32, (8, 128), 1)
    halo_out[:, inner_s:] = jnp.where(
        (lane8 == 0) & jnp.logical_not(low_rows & (my_live > 0.0)), FAR_BIAS, 0.0
    )
    places = [0, 1, 2, 3, 5, 6, 7, 8]
    halo_copies = []
    for index, (inside, target) in enumerate(beside):
        copy = pltpu.make_async_remote_copy(
            src_ref=halo_out,
            dst_ref=halo.at[8 - places[index]],
            send_sem=halo_send.at[index],
            recv_sem=halo_recv.at[7 - index],
            device_id=target,
            device_id_type=MESH_ID,
        )

        @pl.when(inside)
        def send_halo(copy=copy):
            copy.start()

        halo_copies.append(copy)
    halo[4] = halo_out[...]
    slide_query = matmul(slide_in, slide_full(0)).astype(bf).astype(f32)
    slide_heads = inner_s // HDS
    head_lane = lax.div(lax.broadcasted_iota(jnp.int32, (8, inner_s), 1), HDS)
    one_lane = jnp.where(lane8 == 0, math.sqrt(HDS), 0.0)
    query_heads = jnp.concatenate(
        [
            jnp.concatenate([jnp.where(head_lane == head, slide_query, 0.0), one_lane], axis=1)
            for head in range(slide_heads)
        ],
        axis=0,
    ).astype(bf)
    for index, (inside, target) in enumerate(beside):
        arriving = pltpu.make_async_remote_copy(
            src_ref=halo_out,
            dst_ref=halo.at[places[index]],
            send_sem=halo_send.at[index],
            recv_sem=halo_recv.at[index],
            device_id=target,
            device_id_type=MESH_ID,
        )

        @pl.when(inside)
        def take_halo(arriving=arriving):
            arriving.wait_recv()

    lane_wide = lax.broadcasted_iota(jnp.int32, (8, halo.shape[2]), 1)
    near = []
    for place in range(9):
        rows = halo[place]
        if place != 4:
            shut = mask_ref[0, 0, places.index(place)] == 0
            rows = jnp.where((lane_wide == inner_s) & shut, FAR_BIAS, rows)
        near.append(rows)
    near = jnp.concatenate(near, axis=0)
    near_keys = near.astype(bf)
    near_values = jnp.concatenate([near[4:], near[:4]], axis=0)[:, :inner_s].astype(bf)
    slide_scores = contract_rows(query_heads, near_keys) / math.sqrt(HDS)
    slide_peak = jnp.max(slide_scores, axis=1, keepdims=True)
    slide_exp = jnp.exp(slide_scores - slide_peak)
    alive = jnp.concatenate([my_live] * slide_heads, axis=0)
    soft = (
        slide_exp / (jnp.sum(slide_exp, axis=1, keepdims=True) + 1.0 - alive) * alive
    ).astype(bf)
    mix_heads = matmul(soft, near_values)
    slide_mix = sum(
        jnp.where(head_lane == head, mix_heads[8 * head : 8 * head + 8], 0.0)
        for head in range(slide_heads)
    ).astype(bf)
    branch = contract_rows(slide_mix, slide_full(3))
    branch_ref[0] = branch[0:2]
    branch_ref[1] = branch[2:4]

    for copy in started + w_copies + [pair_copy]:
        copy.wait_send()
    for (inside, target), copy in zip(beside, halo_copies):

        @pl.when(inside)
        def sent_halo(copy=copy):
            copy.wait_send()


def halo_lane(halo):
    return halo.shape[2] - 128


def fused(
    tile_tokens,
    tile_count,
    tile_cell,
    occupancy,
    block_mask,
    enc_gain,
    w_query,
    w_key,
    w_value,
    w_out_t,
    final_gain,
    w_proj,
    slide_gain,
    s_query,
    s_key,
    s_value,
    s_out_t,
):
    tiles = lax.axis_size("tile")
    rows_n = lax.axis_size("row")
    cols_n = lax.axis_size("col")
    slots, patch, width = tile_tokens.shape
    inner = w_query.shape[1]
    model = w_proj.shape[1]
    inner_s = s_query.shape[1]
    half = inner // 2
    sizes = (tiles, rows_n, cols_n, slots, patch, width, inner)
    bf, f32 = jnp.bfloat16, jnp.float32
    vmem = pl.BlockSpec(memory_space=pltpu.VMEM)
    smem = pl.BlockSpec(memory_space=pltpu.SMEM)
    slab = pltpu.VMEM((tiles, 8, 256), f32)
    packed = pltpu.VMEM((tiles, 8, half), f32)
    one_packed = pltpu.VMEM((8, half), f32)
    heads_slab = pltpu.VMEM((tiles, 48, 256), bf)
    stat_slab = pltpu.VMEM((tiles, 8, half + 128), f32)

    def kernel(*refs):
        fused_kernel(sizes, *refs)

    return pl.pallas_call(
        kernel,
        out_shape=(
            jax.ShapeDtypeStruct((BLOCK, BLOCK, model), bf),
            jax.ShapeDtypeStruct((BLOCK, BLOCK, model), f32),
        ),
        in_specs=[smem] * 3 + [pl.BlockSpec(memory_space=pl.ANY)] + [vmem] * 12,
        out_specs=(vmem, vmem),
        scratch_shapes=[
            pltpu.VMEM((slots, 16, width), bf),
            pltpu.VMEM((slots, patch, width), bf),
            pltpu.VMEM((slots * patch, width), bf),
            slab,
            slab,
            packed,
            packed,
            one_packed,
            packed,
            heads_slab,
            heads_slab,
            heads_slab,
            heads_slab,
            packed,
            packed,
            one_packed,
            packed,
            stat_slab,
            stat_slab,
            one_packed,
            packed,
            pltpu.VMEM((8, inner_s + 128), f32),
            pltpu.VMEM((9, 8, inner_s + 128), f32),
            pltpu.VMEM((48, width), bf),
            slab,
            pltpu.VMEM((tiles, 8, 128), f32),
            pltpu.VMEM((4, tiles, s_query.shape[0], inner_s), bf),
            pltpu.SemaphoreType.DMA((2,)),
            pltpu.SemaphoreType.DMA((PHASES + 1, tiles)),
            pltpu.SemaphoreType.DMA((PHASES + 1, tiles)),
            pltpu.SemaphoreType.DMA((tiles,)),
            pltpu.SemaphoreType.DMA((tiles,)),
            pltpu.SemaphoreType.DMA((8,)),
            pltpu.SemaphoreType.DMA((8,)),
        ],
        compiler_params=pltpu.CompilerParams(
            collective_id=0, has_side_effects=True, vmem_limit_bytes=48 * 1024 * 1024
        ),
    )(
        tile_cell,
        tile_count,
        block_mask,
        tile_tokens,
        enc_gain.reshape(1, width),
        final_gain.reshape(1, width),
        slide_gain.reshape(1, model),
        w_query,
        w_key,
        w_value,
        w_out_t,
        w_proj,
        s_query,
        s_key,
        s_value,
        s_out_t,
    )


def solution(mesh):
    placed = (
        P(("tile", "row", "col"), None, None),
        P(),
        P(),
        P(),
        P(("tile", "row"), "col", None),
        P(),
        P("tile", None),
        P("tile", None),
        P("tile", None),
        P("tile", None),
        P(),
        P("tile", None),
        P(),
        P("tile", None),
        P("tile", None),
        P("tile", None),
        P("tile", None),
    )
    per_device = fused if fits_fused(mesh) else local
    return jax.shard_map(
        per_device,
        mesh=mesh,
        in_specs=placed,
        out_specs=(P(("tile", "row"), "col", None), P(("tile", "row"), "col", None)),
        check_vma=False,
    )
```

```python
import math

import jax
import jax.numpy as jnp
from jax import lax
from jax.experimental import pallas as pl
from jax.experimental.pallas import tpu as pltpu
from jax.sharding import PartitionSpec as P

HD = 64
HDS = 48
BLOCK = 2


def with_halo(cells, sides, width):
    for axis, dim in sides:
        count = lax.axis_size(axis)
        ends = count - 1
        head = lax.slice_in_dim(cells, 0, width, axis=dim)
        tail = lax.slice_in_dim(cells, cells.shape[dim] - width, cells.shape[dim], axis=dim)
        cells = jnp.concatenate(
            [
                lax.ppermute(tail, axis, [(i, (i + 1) % count) for i in range(ends)]),
                cells,
                lax.ppermute(head, axis, [((i + 1) % count, i) for i in range(ends)]),
            ],
            axis=dim,
        )
    return cells


def layer_norm(vector, scale_gain, epsilon):
    row_mean = jnp.mean(vector, axis=-1, keepdims=True)
    centered = vector - row_mean
    spread = jnp.mean(centered * centered, axis=-1, keepdims=True)
    return centered * lax.rsqrt(spread + epsilon) * scale_gain


def contract_last(first_op, second_op):
    return lax.dot_general(
        first_op,
        second_op,
        (((first_op.ndim - 1,), (1,)), ((), ())),
        preferred_element_type=jnp.float32,
    )


def class_branch(one_tile, query_row, enc_gain, key_part, value_part):
    wide_tile = one_tile.astype(jnp.float32)
    normed = layer_norm(wide_tile, enc_gain, 1e-06).astype(jnp.bfloat16)
    tile_keys = jnp.dot(normed, key_part, preferred_element_type=jnp.float32).astype(jnp.bfloat16)
    tile_values = jnp.dot(normed, value_part, preferred_element_type=jnp.float32).astype(
        jnp.bfloat16
    )
    head_count = key_part.shape[1] // HD
    scores = jnp.einsum(
        "hd,phd->hp",
        query_row.reshape(head_count, HD),
        tile_keys.reshape(-1, head_count, HD),
        preferred_element_type=jnp.float32,
    ) / math.sqrt(HD)
    row_peak = jnp.max(scores, axis=1, keepdims=True)
    weights_exp = jnp.exp(scores - row_peak)
    soft = (weights_exp / jnp.sum(weights_exp, axis=1, keepdims=True)).astype(jnp.bfloat16)
    return (
        jnp.einsum(
            "hp,phd->hd",
            soft,
            tile_values.reshape(-1, head_count, HD),
            preferred_element_type=jnp.float32,
        )
        .reshape(1, -1)
        .astype(jnp.bfloat16)
    )


def partial_rows(buffer, queries, low_row, high_row, weights, out_part):
    enc_gain, key_part, value_part = weights
    row_width = out_part.shape[0]

    def one_slot(slot_index, running):
        one_tile = lax.dynamic_index_in_dim(buffer, slot_index, 0, keepdims=False)
        query_row = lax.dynamic_index_in_dim(queries, slot_index, 0, keepdims=False)
        class_mix = class_branch(one_tile, query_row, enc_gain, key_part, value_part)
        result_row = contract_last(class_mix, out_part)[0]
        return lax.dynamic_update_index_in_dim(running, result_row, slot_index, 0)

    blank_rows = jnp.zeros((buffer.shape[0], row_width), jnp.float32)
    return lax.fori_loop(low_row, high_row, one_slot, blank_rows)


def encode_segment(buffer, queries, low_row, high_row, weights, out_part, final_gain, w_proj):
    partial_value = partial_rows(buffer, queries, low_row, high_row, weights, out_part)
    carried = buffer[:, 0, :].astype(jnp.float32) + partial_value
    final_rows = layer_norm(carried, final_gain, 1e-06).astype(jnp.bfloat16)
    result = jnp.dot(final_rows, w_proj, preferred_element_type=jnp.float32).astype(jnp.bfloat16)
    slot_ids = jnp.arange(buffer.shape[0])
    kept = (slot_ids >= low_row) & (slot_ids < high_row)
    return jnp.where(kept[:, None], result, jnp.zeros_like(result))


def local(
    tile_tokens,
    tile_count,
    tile_cell,
    occupancy,
    block_mask,
    enc_gain,
    w_query,
    w_key,
    w_value,
    w_out_t,
    final_gain,
    w_proj,
    slide_gain,
    s_query,
    s_key,
    s_value,
    s_out_t,
):
    tile_devices = lax.axis_size("tile")
    row_devices = lax.axis_size("row")
    column_devices = lax.axis_size("col")
    tile_index = lax.axis_index("tile")
    row_index = lax.axis_index("row")
    column_index = lax.axis_index("col")
    slot_total = tile_tokens.shape[0]
    counts = tile_count.reshape(tile_devices, row_devices, column_devices)
    class_raw = tile_tokens[:, 0, :]
    key_value = (
        lax.all_gather(w_key, "tile", axis=0, tiled=True),
        lax.all_gather(w_value, "tile", axis=0, tiled=True),
    )
    weights = (enc_gain, key_value[0], key_value[1])
    class_side = (
        lax.all_gather(w_query, "tile", axis=0, tiled=True),
        lax.all_gather(w_out_t, "tile", axis=0, tiled=True),
        lax.all_gather(w_proj, "tile", axis=0, tiled=True),
    )
    own_normed = layer_norm(class_raw.astype(jnp.float32), enc_gain, 1e-06).astype(jnp.bfloat16)
    queries = jnp.dot(own_normed, class_side[0], preferred_element_type=jnp.float32).astype(
        jnp.bfloat16
    )
    out_part = class_side[1]
    full_proj = class_side[2]
    slide_full = (
        lax.all_gather(s_query, "tile", axis=0, tiled=True),
        lax.all_gather(s_key, "tile", axis=0, tiled=True),
        lax.all_gather(s_value, "tile", axis=0, tiled=True),
        lax.all_gather(s_out_t, "tile", axis=0, tiled=True),
    )
    own_count = counts[tile_index, row_index, column_index]
    encoded = encode_segment(
        tile_tokens, queries, 0, own_count, weights, out_part, final_gain, full_proj
    )
    width_model = encoded.shape[1]
    group_cells = tile_cell.reshape(tile_devices, row_devices, column_devices, slot_total)[
        :, row_index, column_index, :
    ]
    live_slots = jnp.arange(slot_total)[None, :] < counts[:, row_index, column_index][:, None]
    grid_cols = BLOCK * column_devices
    grid_row = group_cells // grid_cols
    grid_col = group_cells % grid_cols
    owner_tile = grid_row // BLOCK // row_devices
    local_cell = grid_row % BLOCK * BLOCK + grid_col % BLOCK
    mine_mask = live_slots & (owner_tile == tile_index)
    cell_ids = jnp.arange(BLOCK * BLOCK)
    my_owner = owner_tile[tile_index]
    my_live = live_slots[tile_index]
    selector = ((my_owner[None, :] == jnp.arange(tile_devices)[:, None]) & my_live[None, :]).astype(
        jnp.bfloat16
    )
    outgoing = jnp.dot(selector, encoded, preferred_element_type=jnp.float32).astype(jnp.bfloat16)
    incoming = lax.all_to_all(outgoing, "tile", split_axis=0, concat_axis=0, tiled=True)
    placement = jnp.any(
        (local_cell[None, :, :] == cell_ids[:, None, None]) & mine_mask[None, :, :], axis=2
    ).astype(jnp.bfloat16)
    block_cells = jnp.dot(placement, incoming, preferred_element_type=jnp.float32)
    grid_tokens = block_cells.astype(jnp.bfloat16).reshape(BLOCK, BLOCK, width_model)
    slide_in = layer_norm(block_cells, slide_gain, 1e-05).astype(jnp.bfloat16)
    slide_query = jnp.dot(slide_in, slide_full[0], preferred_element_type=jnp.float32).astype(
        jnp.bfloat16
    )
    slide_keys = jnp.dot(slide_in, slide_full[1], preferred_element_type=jnp.float32).astype(
        jnp.bfloat16
    )
    slide_values = jnp.dot(slide_in, slide_full[2], preferred_element_type=jnp.float32).astype(
        jnp.bfloat16
    )
    inner_width = slide_keys.shape[1]
    key_value_cells = jnp.concatenate([slide_keys, slide_values], axis=1).reshape(
        BLOCK, BLOCK, 2 * inner_width
    )
    surround = with_halo(key_value_cells, ((("tile", "row"), 0), ("col", 1)), BLOCK)
    near_rows = surround.reshape(-1, 2 * inner_width)
    near_keys = near_rows[:, :inner_width]
    near_values = near_rows[:, inner_width:]
    block_row = tile_index * row_devices + row_index
    padded = jnp.pad(occupancy, BLOCK)
    window = lax.dynamic_slice(
        padded, (block_row * BLOCK, column_index * BLOCK), (3 * BLOCK, 3 * BLOCK)
    )
    mask_row = block_mask.reshape(-1)
    mask_grid = jnp.concatenate([mask_row[:4], jnp.ones((1,), jnp.int32), mask_row[4:]]).reshape(
        3, 3
    )
    mask_cells = jnp.repeat(jnp.repeat(mask_grid, BLOCK, axis=0), BLOCK, axis=1)
    usable = (window * mask_cells).reshape(-1) > 0
    query_live = (
        lax.dynamic_slice(occupancy, (block_row * BLOCK, column_index * BLOCK), (BLOCK, BLOCK))
        .reshape(-1)
        .astype(jnp.float32)
    )
    head_count = inner_width // HDS
    scores = jnp.einsum(
        "qhd,khd->hqk",
        slide_query.reshape(-1, head_count, HDS),
        near_keys.reshape(-1, head_count, HDS),
        preferred_element_type=jnp.float32,
    ) / math.sqrt(HDS)
    allow = usable[None, None, :]
    row_peak = jnp.max(jnp.where(allow, scores, -1e30), axis=-1, keepdims=True)
    weights_exp = jnp.where(allow, jnp.exp(scores - row_peak), 0.0)
    live_query = query_live[None, :, None]
    soft = (
        weights_exp / (jnp.sum(weights_exp, axis=-1, keepdims=True) + 1.0 - live_query) * live_query
    ).astype(jnp.bfloat16)
    slide_mix = (
        jnp.einsum(
            "hqk,khd->qhd",
            soft,
            near_values.reshape(-1, head_count, HDS),
            preferred_element_type=jnp.float32,
        )
        .reshape(-1, inner_width)
        .astype(jnp.bfloat16)
    )
    slide_branch = contract_last(slide_mix, slide_full[3]).reshape(BLOCK, BLOCK, width_model)
    return (grid_tokens, slide_branch)


MESH_ID = pl.DeviceIdType.MESH
NEAR = [(-1, -1), (-1, 0), (-1, 1), (0, -1), (0, 1), (1, -1), (1, 0), (1, 1)]
FAR_BIAS = -1e30
PHASES = 8


def fits_fused(mesh):
    return (mesh.shape["tile"], mesh.shape["row"], mesh.shape["col"]) == (8, 2, 2)


def contract_rows(first_op, second_op):
    return lax.dot_general(
        first_op, second_op, (((1,), (1,)), ((), ())), preferred_element_type=jnp.float32
    )


def matmul(first_op, second_op):
    return jnp.dot(first_op, second_op, preferred_element_type=jnp.float32)


def fused_kernel(
    sizes,
    cell_ref,
    count_ref,
    mask_ref,
    tok_hbm,
    enc_gain_hbm,
    final_gain_hbm,
    slide_gain_hbm,
    wq_hbm,
    wk_hbm,
    wv_hbm,
    wo_hbm,
    wp_hbm,
    sq_hbm,
    sk_hbm,
    sv_hbm,
    so_hbm,
    grid_ref,
    branch_ref,
    cls,
    tok,
    normed,
    s1,
    r1,
    s2,
    r2,
    s3,
    r3,
    s4,
    r4,
    s5,
    r5,
    s6,
    r6,
    s7,
    r7,
    s9,
    r9,
    sg,
    rg,
    halo_out,
    halo,
    wide,
    gains,
    live,
    slide_w,
    wq_ref,
    wk_ref,
    wv_ref,
    wo_ref,
    wp_ref,
    enc_gain_ref,
    final_gain_ref,
    slide_gain_ref,
    in_sem,
    send_sem,
    recv_sem,
    w_send,
    w_recv,
    halo_send,
    halo_recv,
):
    tiles, rows_n, cols_n, slots, patch, width, inner = sizes
    shard = width // tiles
    half = inner // 2
    heads = inner // HD
    third = inner // slots
    third_heads = heads // slots
    bf, f32 = jnp.bfloat16, jnp.float32
    me = lax.axis_index("tile")
    my_row = lax.axis_index("row")
    my_col = lax.axis_index("col")
    block_row = me * rows_n + my_row

    first_in = pltpu.make_async_copy(tok_hbm.at[:, pl.ds(0, 16), :], cls, in_sem.at[0])
    first_in.start()
    whole_in = pltpu.make_async_copy(tok_hbm, tok, in_sem.at[1])
    gain_ins = []
    for place, (source, landing) in enumerate(
        (
            (enc_gain_hbm, enc_gain_ref),
            (final_gain_hbm, final_gain_ref),
            (slide_gain_hbm, slide_gain_ref),
        )
    ):
        gain_ins.append(pltpu.make_async_copy(source, landing, in_sem.at[2 + place]))
        gain_ins[-1].start()
    weight_ins = []
    for place, (source, landing) in enumerate(
        ((wq_hbm, wq_ref), (wp_hbm, wp_ref), (wk_hbm, wk_ref), (wv_hbm, wv_ref), (wo_hbm, wo_ref))
    ):
        weight_ins.append(pltpu.make_async_copy(source, landing, in_sem.at[5 + place]))
    wq_in, wp_in, wk_in, wv_in, wo_in = weight_ins
    wq_in.start()
    mine = my_row * 2 + my_col
    own_pair = pl.ds(my_row * 2, 2)
    for which, source in enumerate((sq_hbm, sk_hbm, sv_hbm, so_hbm)):

        @pl.when(mine == which)
        def bring(source=source):
            pltpu.make_async_copy(source, slide_w.at[mine, me], in_sem.at[10]).start()

    own_in = pltpu.make_async_copy(sq_hbm, slide_w.at[mine, me], in_sem.at[10])
    wp_in.start()
    whole_in.start()
    for copy in (wk_in, wv_in, wo_in):
        copy.start()

    blank = jnp.where(
        lax.broadcasted_iota(jnp.int32, (8, halo.shape[2]), 1) == halo_lane(halo), FAR_BIAS, 0.0
    )
    for place in range(9):
        halo[place] = blank

    barrier = pltpu.get_barrier_semaphore()
    for step in range(1, tiles):
        pl.semaphore_signal(
            barrier, inc=1, device_id={"tile": lax.rem(me + step, tiles)}, device_id_type=MESH_ID
        )
    beside = []
    near_count = jnp.int32(0)
    for down, right in NEAR:
        to_row = block_row + down
        to_col = my_col + right
        inside = (to_row >= 0) & (to_row < tiles * rows_n) & (to_col >= 0) & (to_col < cols_n)
        target = {
            "tile": lax.div(to_row + rows_n, rows_n) - 1,
            "row": lax.rem(to_row + rows_n, rows_n),
            "col": to_col,
        }
        beside.append((inside, target))
        near_count = near_count + inside.astype(jnp.int32)

        @pl.when(inside)
        def greet(target=target):
            pl.semaphore_signal(barrier, inc=1, device_id=target, device_id_type=MESH_ID)

    first_in.wait()
    raw = [cls[slot].astype(f32)[0:1] for slot in range(slots)]
    raw_rows = jnp.concatenate(raw, axis=0)
    for copy in gain_ins:
        copy.wait()
    enc_gain = enc_gain_ref[...].reshape(1, width)
    final_gain = final_gain_ref[...].reshape(1, width)
    class_normed = layer_norm(raw_rows, enc_gain, 1e-06).astype(bf).astype(f32)
    class_rows = jnp.concatenate(
        [class_normed] * 3 + [raw_rows, jnp.zeros((16 - 4 * slots, width), f32)], axis=0
    ).astype(bf)
    for to in range(tiles):
        s1[to, :, :shard] = class_rows[:, to * shard : (to + 1) * shard]
        gains[to, :, :shard] = jnp.broadcast_to(
            final_gain[:, to * shard : (to + 1) * shard], (8, shard)
        )

    pl.semaphore_wait(barrier, tiles - 1 + near_count)

    started = []

    def send(phase, source, landing):
        copies = []
        for step in range(1, tiles):
            to = lax.rem(me + step, tiles)
            copy = pltpu.make_async_remote_copy(
                src_ref=source.at[to] if len(source.shape) == len(landing.shape) else source,
                dst_ref=landing.at[me],
                send_sem=send_sem.at[phase, step],
                recv_sem=recv_sem.at[phase, step],
                device_id={"tile": to},
                device_id_type=MESH_ID,
            )
            copy.start()
            copies.append(copy)
        started.extend(copies)
        landing[me] = source[me] if len(source.shape) == len(landing.shape) else source[...]
        return copies

    def arrive(copies):
        for copy in copies:
            copy.wait_recv()

    copies1 = send(0, s1, r1)

    own_in.wait()

    def relay_copy(hop, side):
        onward = 2 if side == 0 else -2
        held = me - onward * hop
        return pltpu.make_async_remote_copy(
            src_ref=slide_w.at[mine, held],
            dst_ref=slide_w.at[mine, held],
            send_sem=w_send.at[side, hop],
            recv_sem=w_recv.at[side, hop],
            device_id={"tile": me + onward},
            device_id_type=MESH_ID,
        )

    def relay_inside(place):
        return (place >= 0) & (place < tiles)

    def relay_send(hop):
        for side, onward in ((0, 2), (1, -2)):

            @pl.when(relay_inside(me + onward) & relay_inside(me - onward * hop))
            def go(side=side):
                relay_copy(hop, side).start()

    def relay_sent(hop):
        for side, onward in ((0, 2), (1, -2)):

            @pl.when(relay_inside(me + onward) & relay_inside(me - onward * hop))
            def done(side=side):
                relay_copy(hop, side).wait_send()

    def relay_take(hop):
        for side, onward in ((0, 2), (1, -2)):
            held = me - onward * (hop + 1)

            @pl.when(relay_inside(held))
            def take(side=side, onward=onward, held=held):
                pltpu.make_async_remote_copy(
                    src_ref=slide_w.at[mine, held],
                    dst_ref=slide_w.at[mine, held],
                    send_sem=w_send.at[side, hop],
                    recv_sem=w_recv.at[side, hop],
                    device_id={"tile": me - onward},
                    device_id_type=MESH_ID,
                ).wait_recv()

    side_y = lax.rem(me, 2)
    lines = tiles // 2

    def across(place, parity):
        shard_at = place * 2 + parity
        return pltpu.make_async_remote_copy(
            src_ref=slide_w.at[mine, shard_at],
            dst_ref=slide_w.at[mine, shard_at],
            send_sem=w_send.at[2, place],
            recv_sem=w_recv.at[2, place],
            device_id={"tile": me + 1 - 2 * side_y},
            device_id_type=MESH_ID,
        )

    over_x = pltpu.make_async_remote_copy(
        src_ref=slide_w.at[mine],
        dst_ref=slide_w.at[mine],
        send_sem=w_send.at[3, 0],
        recv_sem=w_recv.at[3, 0],
        device_id={"col": 1 - my_col},
        device_id_type=MESH_ID,
    )
    pair_copy = pltpu.make_async_remote_copy(
        src_ref=slide_w.at[own_pair],
        dst_ref=slide_w.at[own_pair],
        send_sem=w_send.at[3, 1],
        recv_sem=w_recv.at[3, 1],
        device_id={"row": 1 - my_row},
        device_id_type=MESH_ID,
    )
    relay_send(0)

    row64 = lax.broadcasted_iota(jnp.int32, (8 * tiles, 1), 0)
    in_block = lax.rem(row64, 8)

    def norm_chunk(chunk, carry):
        rows = pl.ds(pl.multiple_of(chunk * 32, 32), 32)
        inside = pl.ds(pl.multiple_of(lax.rem(chunk, per_tile) * 32, 32), 32)
        wide_rows_in = tok[lax.div(chunk, per_tile), inside, :].astype(f32)
        normed[rows, :] = layer_norm(wide_rows_in, enc_gain, 1e-06).astype(bf)
        return carry

    per_tile = patch // 32
    whole_chunks = slots * per_tile
    whole_in.wait()
    my_gain = gains[me][:, :shard]
    wp_in.wait()
    gain_high = my_gain.astype(bf)
    gain_low = (my_gain - gain_high.astype(f32)).astype(bf)
    sums = [
        matmul(gain_high, wp_ref[:, cut : cut + half])
        + matmul(gain_low, wp_ref[:, cut : cut + half])
        for cut in (0, half)
    ]
    low_rows = lax.broadcasted_iota(jnp.int32, (8, 1), 0) < 4
    sg[...] = jnp.where(low_rows, sums[0], sums[1])

    col64 = lax.broadcasted_iota(jnp.int32, (8 * tiles, 16 * tiles), 1)
    row_full = lax.broadcasted_iota(jnp.int32, (8 * tiles, 16 * tiles), 0)
    place_low = jnp.zeros((8 * tiles, 16 * tiles), f32)
    grid_cols = BLOCK * cols_n
    group = my_row * cols_n + my_col
    row_key = lax.div(row_full, 8) * 4 + lax.rem(row_full, 4)
    for other in range(tiles):
        device = other * rows_n * cols_n + group
        count = count_ref[device]
        for slot in range(slots):
            cell = cell_ref[device * slots + slot]
            cell_row = lax.div(cell, jnp.int32(grid_cols))
            cell_col = lax.rem(cell, jnp.int32(grid_cols))
            owner = lax.div(cell_row, jnp.int32(BLOCK * rows_n))
            spot = owner * 4 + lax.rem(cell_row, BLOCK) * BLOCK + lax.rem(cell_col, BLOCK)
            spot = jnp.where(slot < count, spot, -1)
            hit = (row_key == spot) & (col64 == other * 16 + slot)
            place_low = jnp.where(hit, 1.0, place_low)
    placing = [
        jnp.concatenate(
            [jnp.zeros((8 * tiles, slots * turn), f32), place_low[:, : -slots * turn]], axis=1
        ).astype(bf)
        for turn in range(1, 4)
    ]
    live_col = jnp.sum(place_low, axis=1, keepdims=True)
    live[...] = jnp.broadcast_to(live_col, (8 * tiles, 128)).reshape(tiles, 8, 128)
    placing.insert(0, place_low.astype(bf))

    arrive(copies1)
    wq_in.wait()
    shards1 = r1[...].reshape(16 * tiles, r1.shape[2])[:, :shard]
    in_wide = lax.rem(lax.broadcasted_iota(jnp.int32, (16 * tiles, 1), 0), 16)
    parts = [matmul(shards1, wq_ref[:, third * k : third * (k + 1)]) for k in range(3)]
    packed_part = jnp.where(
        in_wide < slots, parts[0], jnp.where(in_wide < 2 * slots, parts[1], parts[2])
    )
    s2[...] = packed_part.astype(bf).reshape(s2.shape)
    copies2 = send(1, s2, r2)
    relay_take(0)
    relay_send(1)
    lax.fori_loop(0, whole_chunks // 3, norm_chunk, 0)
    arrive(copies2)
    s3[...] = jnp.sum(r2[...].astype(f32), axis=0).astype(bf)
    copies3 = send(2, s3, r3)
    relay_take(1)
    relay_send(2)
    lax.fori_loop(whole_chunks // 3, 2 * (whole_chunks // 3), norm_chunk, 0)

    wide_rows = 48 * tiles
    exp_row = lax.broadcasted_iota(jnp.int32, (wide_rows, 16 * tiles), 0)
    exp_col = lax.broadcasted_iota(jnp.int32, (wide_rows, 16 * tiles), 1)
    exp_in = lax.rem(exp_row, 48)
    exp_slot = lax.div(exp_in, heads)
    exp_head = lax.rem(exp_in, heads)
    exp_turn = lax.div(exp_head, third_heads)
    exp_base = lax.div(exp_row, 48) * 16 + exp_turn * slots + exp_slot
    pick = ((exp_slot < slots) & (exp_col == exp_base)).astype(f32).astype(bf)
    head_of_row = lax.rem(
        lax.rem(lax.broadcasted_iota(jnp.int32, (wide_rows, third), 0), 48), heads
    )
    head_of_col = lax.div(lax.broadcasted_iota(jnp.int32, (wide_rows, third), 1), HD)
    own = [head_of_row == head_of_col + turn * third_heads for turn in range(3)]
    arrive(copies3)
    wk_in.wait()
    queries = matmul(pick, r3[...].reshape(16 * tiles, third))
    query_wide = jnp.concatenate([jnp.where(at, queries, 0.0) for at in own], axis=1).astype(bf)
    folded = contract_rows(query_wide, wk_ref[...])
    s4[:, :, :shard] = folded.astype(bf).reshape(tiles, 48, shard)
    copies4 = send(3, s4, r4)
    lax.fori_loop(2 * (whole_chunks // 3), whole_chunks, norm_chunk, 0)
    arrive(copies4)
    copies_g = send(7, sg, rg)
    relay_take(2)
    for place in range(lines):
        across(place, side_y).start()

    for other in range(tiles):
        wide[:, other * shard : (other + 1) * shard] = r4[other, :, :shard]
    tokens = normed[...]
    scores = contract_rows(wide[...], tokens) / math.sqrt(HD)
    score_slot = lax.div(lax.broadcasted_iota(jnp.int32, scores.shape, 0), heads)
    score_tile = lax.div(lax.broadcasted_iota(jnp.int32, scores.shape, 1), patch)
    same = score_slot == score_tile
    peak = jnp.max(jnp.where(same, scores, -1e30), axis=1, keepdims=True)
    grown = jnp.where(same, jnp.exp(jnp.minimum(scores - peak, 0.0)), 0.0)
    total = jnp.sum(grown, axis=1, keepdims=True)
    probs = (grown / jnp.where(total > 0.0, total, 1.0)).astype(bf)
    mixed = matmul(probs, tokens).astype(bf)
    for to in range(tiles):
        s5[to, :, :shard] = mixed[:, to * shard : (to + 1) * shard]
    copies5 = send(4, s5, r5)
    for place in range(lines):
        across(place, 1 - side_y).wait_recv()
    over_x.start()
    arrive(copies5)
    wv_in.wait()

    mixes = r5[...].reshape(wide_rows, r5.shape[2])[:, :shard]
    valued = jnp.zeros((wide_rows, third), f32)
    for turn in range(3):
        columns = wv_ref[:, third * turn : third * (turn + 1)]
        valued = jnp.where(own[turn], matmul(mixes, columns), valued)
    gathered = lax.dot_general(
        pick, valued.astype(bf), (((0,), (0,)), ((), ())), preferred_element_type=f32
    ).astype(bf)
    s6[...] = gathered.reshape(s6.shape)
    copies6 = send(5, s6, r6)
    arrive(copies6)
    s7[...] = jnp.sum(r6[...].astype(f32), axis=0).astype(bf)
    copies7 = send(6, s7, r7)
    raw_cells = matmul(placing[3], shards1)

    arrive(copies7)
    wo_in.wait()

    mix_rows = r7[...].reshape(16 * tiles, third)
    cell_mix = jnp.concatenate([matmul(placing[k], mix_rows) for k in range(3)], axis=1)
    carried = raw_cells + contract_rows(cell_mix.astype(bf), wo_ref[...])
    part_mean = jnp.mean(carried, axis=1, keepdims=True)
    centered = carried - part_mean
    part_square = jnp.sum(centered * centered, axis=1, keepdims=True)
    scaled = (centered * my_gain[0:1]).astype(bf)
    landed = jnp.where(
        in_block < 4, matmul(scaled, wp_ref[:, :half]), matmul(scaled, wp_ref[:, half:])
    )
    s9[:, :, :half] = landed.reshape(tiles, 8, half)
    lane = lax.broadcasted_iota(jnp.int32, (8 * tiles, 128), 1)
    s9[:, :, half:] = jnp.where(lane == 0, part_mean, part_square).reshape(tiles, 8, 128)
    copies9 = send(8, s9, r9)
    over_x.wait_recv()
    pair_copy.start()
    arrive(copies_g)
    arrive(copies9)

    means = [r9[other, :, half : half + 1] for other in range(tiles)]
    mean = sum(means) / tiles
    square = sum(
        r9[other, :, half + 1 : half + 2] + shard * (means[other] - mean) ** 2
        for other in range(tiles)
    )
    joined = sum(
        r9[other, :, :half] + (means[other] - mean) * rg[other] for other in range(tiles)
    )
    joined = (joined * lax.rsqrt(square / width + 1e-06)).astype(bf)
    cells32 = joined.astype(f32)
    cells = jnp.concatenate([cells32[0:4], cells32[4:8]], axis=1)
    grid_ref[0] = cells[0:2].astype(bf)
    grid_ref[1] = cells[2:4].astype(bf)

    pair_copy.wait_recv()
    inner_s = slide_w.shape[3]
    slide_rows = jnp.concatenate([cells, cells], axis=0)
    slide_in = layer_norm(slide_rows, slide_gain_ref[...].reshape(1, -1), 1e-05).astype(bf)

    def slide_full(which):
        return slide_w[which].reshape(-1, inner_s)

    keys = matmul(slide_in, slide_full(1))
    values = matmul(slide_in, slide_full(2))
    my_live = live[me][:, 0:1]
    halo_out[:, :inner_s] = jnp.where(low_rows, keys, values).astype(bf).astype(f32)
    lane8 = lax.broadcasted_iota(jnp.int32, (8, 128), 1)
    halo_out[:, inner_s:] = jnp.where(
        (lane8 == 0) & jnp.logical_not(low_rows & (my_live > 0.0)), FAR_BIAS, 0.0
    )
    places = [0, 1, 2, 3, 5, 6, 7, 8]
    halo_copies = []
    for index, (inside, target) in enumerate(beside):
        copy = pltpu.make_async_remote_copy(
            src_ref=halo_out,
            dst_ref=halo.at[8 - places[index]],
            send_sem=halo_send.at[index],
            recv_sem=halo_recv.at[7 - index],
            device_id=target,
            device_id_type=MESH_ID,
        )

        @pl.when(inside)
        def send_halo(copy=copy):
            copy.start()

        halo_copies.append(copy)
    halo[4] = halo_out[...]
    slide_query = matmul(slide_in, slide_full(0)).astype(bf).astype(f32)
    slide_heads = inner_s // HDS
    head_lane = lax.div(lax.broadcasted_iota(jnp.int32, (8, inner_s), 1), HDS)
    one_lane = jnp.where(lane8 == 0, math.sqrt(HDS), 0.0)
    query_heads = jnp.concatenate(
        [
            jnp.concatenate([jnp.where(head_lane == head, slide_query, 0.0), one_lane], axis=1)
            for head in range(slide_heads)
        ],
        axis=0,
    ).astype(bf)
    for index, (inside, target) in enumerate(beside):
        arriving = pltpu.make_async_remote_copy(
            src_ref=halo_out,
            dst_ref=halo.at[places[index]],
            send_sem=halo_send.at[index],
            recv_sem=halo_recv.at[index],
            device_id=target,
            device_id_type=MESH_ID,
        )

        @pl.when(inside)
        def take_halo(arriving=arriving):
            arriving.wait_recv()

    lane_wide = lax.broadcasted_iota(jnp.int32, (8, halo.shape[2]), 1)
    near = []
    for place in range(9):
        rows = halo[place]
        if place != 4:
            shut = mask_ref[0, 0, places.index(place)] == 0
            rows = jnp.where((lane_wide == inner_s) & shut, FAR_BIAS, rows)
        near.append(rows)
    near = jnp.concatenate(near, axis=0)
    near_keys = near.astype(bf)
    near_values = jnp.concatenate([near[4:], near[:4]], axis=0)[:, :inner_s].astype(bf)
    slide_scores = contract_rows(query_heads, near_keys) / math.sqrt(HDS)
    slide_peak = jnp.max(slide_scores, axis=1, keepdims=True)
    slide_exp = jnp.exp(slide_scores - slide_peak)
    alive = jnp.concatenate([my_live] * slide_heads, axis=0)
    soft = (
        slide_exp / (jnp.sum(slide_exp, axis=1, keepdims=True) + 1.0 - alive) * alive
    ).astype(bf)
    mix_heads = matmul(soft, near_values)
    slide_mix = sum(
        jnp.where(head_lane == head, mix_heads[8 * head : 8 * head + 8], 0.0)
        for head in range(slide_heads)
    ).astype(bf)
    branch = contract_rows(slide_mix, slide_full(3))
    branch_ref[0] = branch[0:2]
    branch_ref[1] = branch[2:4]

    for copy in started + [across(place, side_y) for place in range(lines)] + [over_x, pair_copy]:
        copy.wait_send()
    for hop in range(3):
        relay_sent(hop)
    for (inside, target), copy in zip(beside, halo_copies):

        @pl.when(inside)
        def sent_halo(copy=copy):
            copy.wait_send()


def halo_lane(halo):
    return halo.shape[2] - 128


def fused(
    tile_tokens,
    tile_count,
    tile_cell,
    occupancy,
    block_mask,
    enc_gain,
    w_query,
    w_key,
    w_value,
    w_out_t,
    final_gain,
    w_proj,
    slide_gain,
    s_query,
    s_key,
    s_value,
    s_out_t,
):
    tiles = lax.axis_size("tile")
    rows_n = lax.axis_size("row")
    cols_n = lax.axis_size("col")
    slots, patch, width = tile_tokens.shape
    inner = w_query.shape[1]
    model = w_proj.shape[1]
    inner_s = s_query.shape[1]
    half = inner // 2
    sizes = (tiles, rows_n, cols_n, slots, patch, width, inner)
    bf, f32 = jnp.bfloat16, jnp.float32
    vmem = pl.BlockSpec(memory_space=pltpu.VMEM)
    smem = pl.BlockSpec(memory_space=pltpu.SMEM)
    slab = pltpu.VMEM((tiles, 16, 256), bf)
    thirds = pltpu.VMEM((tiles, 16, inner // 3), bf)
    one_third = pltpu.VMEM((16, inner // 3), bf)
    packed = pltpu.VMEM((tiles, 8, half), f32)
    one_packed = pltpu.VMEM((8, half), f32)
    heads_slab = pltpu.VMEM((tiles, 48, 256), bf)
    stat_slab = pltpu.VMEM((tiles, 8, half + 128), f32)

    def kernel(*refs):
        fused_kernel(sizes, *refs)

    return pl.pallas_call(
        kernel,
        out_shape=(
            jax.ShapeDtypeStruct((BLOCK, BLOCK, model), bf),
            jax.ShapeDtypeStruct((BLOCK, BLOCK, model), f32),
        ),
        in_specs=[smem] * 3 + [pl.BlockSpec(memory_space=pl.ANY)] * 13,
        out_specs=(vmem, vmem),
        scratch_shapes=[
            pltpu.VMEM((slots, 16, width), bf),
            pltpu.VMEM((slots, patch, width), bf),
            pltpu.VMEM((slots * patch, width), bf),
            slab,
            slab,
            thirds,
            thirds,
            one_third,
            thirds,
            heads_slab,
            heads_slab,
            heads_slab,
            heads_slab,
            thirds,
            thirds,
            one_third,
            thirds,
            stat_slab,
            stat_slab,
            one_packed,
            packed,
            pltpu.VMEM((8, inner_s + 128), f32),
            pltpu.VMEM((9, 8, inner_s + 128), f32),
            pltpu.VMEM((48, width), bf),
            pltpu.VMEM((tiles, 8, 256), f32),
            pltpu.VMEM((tiles, 8, 128), f32),
            pltpu.VMEM((4, tiles, s_query.shape[0], inner_s), bf),
            pltpu.VMEM(w_query.shape, bf),
            pltpu.VMEM(w_key.shape, bf),
            pltpu.VMEM(w_value.shape, bf),
            pltpu.VMEM(w_out_t.shape, bf),
            pltpu.VMEM(w_proj.shape, bf),
            pltpu.VMEM((width,), f32),
            pltpu.VMEM((width,), f32),
            pltpu.VMEM((model,), f32),
            pltpu.SemaphoreType.DMA((12,)),
            pltpu.SemaphoreType.DMA((PHASES + 1, tiles)),
            pltpu.SemaphoreType.DMA((PHASES + 1, tiles)),
            pltpu.SemaphoreType.DMA((4, tiles)),
            pltpu.SemaphoreType.DMA((4, tiles)),
            pltpu.SemaphoreType.DMA((8,)),
            pltpu.SemaphoreType.DMA((8,)),
        ],
        compiler_params=pltpu.CompilerParams(
            collective_id=0, has_side_effects=True, vmem_limit_bytes=60 * 1024 * 1024
        ),
    )(
        tile_cell,
        tile_count,
        block_mask,
        tile_tokens,
        enc_gain,
        final_gain,
        slide_gain,
        w_query,
        w_key,
        w_value,
        w_out_t,
        w_proj,
        s_query,
        s_key,
        s_value,
        s_out_t,
    )


def solution(mesh):
    placed = (
        P(("tile", "row", "col"), None, None),
        P(),
        P(),
        P(),
        P(("tile", "row"), "col", None),
        P(),
        P("tile", None),
        P("tile", None),
        P("tile", None),
        P("tile", None),
        P(),
        P("tile", None),
        P(),
        P("tile", None),
        P("tile", None),
        P("tile", None),
        P("tile", None),
    )
    per_device = fused if fits_fused(mesh) else local
    return jax.shard_map(
        per_device,
        mesh=mesh,
        in_specs=placed,
        out_specs=(P(("tile", "row"), "col", None), P(("tile", "row"), "col", None)),
        check_vma=False,
    )
```

```python
import math

import jax
import jax.numpy as jnp
from jax import lax
from jax.experimental import pallas as pl
from jax.experimental.pallas import tpu as pltpu
from jax.sharding import PartitionSpec as P

HD = 64
HDS = 48
BLOCK = 2


def with_halo(cells, sides, width):
    for axis, dim in sides:
        count = lax.axis_size(axis)
        ends = count - 1
        head = lax.slice_in_dim(cells, 0, width, axis=dim)
        tail = lax.slice_in_dim(cells, cells.shape[dim] - width, cells.shape[dim], axis=dim)
        cells = jnp.concatenate(
            [
                lax.ppermute(tail, axis, [(i, (i + 1) % count) for i in range(ends)]),
                cells,
                lax.ppermute(head, axis, [((i + 1) % count, i) for i in range(ends)]),
            ],
            axis=dim,
        )
    return cells


def layer_norm(vector, scale_gain, epsilon):
    row_mean = jnp.mean(vector, axis=-1, keepdims=True)
    centered = vector - row_mean
    spread = jnp.mean(centered * centered, axis=-1, keepdims=True)
    return centered * lax.rsqrt(spread + epsilon) * scale_gain


def contract_last(first_op, second_op):
    return lax.dot_general(
        first_op,
        second_op,
        (((first_op.ndim - 1,), (1,)), ((), ())),
        preferred_element_type=jnp.float32,
    )


def class_branch(one_tile, query_row, enc_gain, key_part, value_part):
    wide_tile = one_tile.astype(jnp.float32)
    normed = layer_norm(wide_tile, enc_gain, 1e-06).astype(jnp.bfloat16)
    tile_keys = jnp.dot(normed, key_part, preferred_element_type=jnp.float32).astype(jnp.bfloat16)
    tile_values = jnp.dot(normed, value_part, preferred_element_type=jnp.float32).astype(
        jnp.bfloat16
    )
    head_count = key_part.shape[1] // HD
    scores = jnp.einsum(
        "hd,phd->hp",
        query_row.reshape(head_count, HD),
        tile_keys.reshape(-1, head_count, HD),
        preferred_element_type=jnp.float32,
    ) / math.sqrt(HD)
    row_peak = jnp.max(scores, axis=1, keepdims=True)
    weights_exp = jnp.exp(scores - row_peak)
    soft = (weights_exp / jnp.sum(weights_exp, axis=1, keepdims=True)).astype(jnp.bfloat16)
    return (
        jnp.einsum(
            "hp,phd->hd",
            soft,
            tile_values.reshape(-1, head_count, HD),
            preferred_element_type=jnp.float32,
        )
        .reshape(1, -1)
        .astype(jnp.bfloat16)
    )


def partial_rows(buffer, queries, low_row, high_row, weights, out_part):
    enc_gain, key_part, value_part = weights
    row_width = out_part.shape[0]

    def one_slot(slot_index, running):
        one_tile = lax.dynamic_index_in_dim(buffer, slot_index, 0, keepdims=False)
        query_row = lax.dynamic_index_in_dim(queries, slot_index, 0, keepdims=False)
        class_mix = class_branch(one_tile, query_row, enc_gain, key_part, value_part)
        result_row = contract_last(class_mix, out_part)[0]
        return lax.dynamic_update_index_in_dim(running, result_row, slot_index, 0)

    blank_rows = jnp.zeros((buffer.shape[0], row_width), jnp.float32)
    return lax.fori_loop(low_row, high_row, one_slot, blank_rows)


def encode_segment(buffer, queries, low_row, high_row, weights, out_part, final_gain, w_proj):
    partial_value = partial_rows(buffer, queries, low_row, high_row, weights, out_part)
    carried = buffer[:, 0, :].astype(jnp.float32) + partial_value
    final_rows = layer_norm(carried, final_gain, 1e-06).astype(jnp.bfloat16)
    result = jnp.dot(final_rows, w_proj, preferred_element_type=jnp.float32).astype(jnp.bfloat16)
    slot_ids = jnp.arange(buffer.shape[0])
    kept = (slot_ids >= low_row) & (slot_ids < high_row)
    return jnp.where(kept[:, None], result, jnp.zeros_like(result))


def local(
    tile_tokens,
    tile_count,
    tile_cell,
    occupancy,
    block_mask,
    enc_gain,
    w_query,
    w_key,
    w_value,
    w_out_t,
    final_gain,
    w_proj,
    slide_gain,
    s_query,
    s_key,
    s_value,
    s_out_t,
):
    tile_devices = lax.axis_size("tile")
    row_devices = lax.axis_size("row")
    column_devices = lax.axis_size("col")
    tile_index = lax.axis_index("tile")
    row_index = lax.axis_index("row")
    column_index = lax.axis_index("col")
    slot_total = tile_tokens.shape[0]
    counts = tile_count.reshape(tile_devices, row_devices, column_devices)
    class_raw = tile_tokens[:, 0, :]
    key_value = (
        lax.all_gather(w_key, "tile", axis=0, tiled=True),
        lax.all_gather(w_value, "tile", axis=0, tiled=True),
    )
    weights = (enc_gain, key_value[0], key_value[1])
    class_side = (
        lax.all_gather(w_query, "tile", axis=0, tiled=True),
        lax.all_gather(w_out_t, "tile", axis=0, tiled=True),
        lax.all_gather(w_proj, "tile", axis=0, tiled=True),
    )
    own_normed = layer_norm(class_raw.astype(jnp.float32), enc_gain, 1e-06).astype(jnp.bfloat16)
    queries = jnp.dot(own_normed, class_side[0], preferred_element_type=jnp.float32).astype(
        jnp.bfloat16
    )
    out_part = class_side[1]
    full_proj = class_side[2]
    slide_full = (
        lax.all_gather(s_query, "tile", axis=0, tiled=True),
        lax.all_gather(s_key, "tile", axis=0, tiled=True),
        lax.all_gather(s_value, "tile", axis=0, tiled=True),
        lax.all_gather(s_out_t, "tile", axis=0, tiled=True),
    )
    own_count = counts[tile_index, row_index, column_index]
    encoded = encode_segment(
        tile_tokens, queries, 0, own_count, weights, out_part, final_gain, full_proj
    )
    width_model = encoded.shape[1]
    group_cells = tile_cell.reshape(tile_devices, row_devices, column_devices, slot_total)[
        :, row_index, column_index, :
    ]
    live_slots = jnp.arange(slot_total)[None, :] < counts[:, row_index, column_index][:, None]
    grid_cols = BLOCK * column_devices
    grid_row = group_cells // grid_cols
    grid_col = group_cells % grid_cols
    owner_tile = grid_row // BLOCK // row_devices
    local_cell = grid_row % BLOCK * BLOCK + grid_col % BLOCK
    mine_mask = live_slots & (owner_tile == tile_index)
    cell_ids = jnp.arange(BLOCK * BLOCK)
    my_owner = owner_tile[tile_index]
    my_live = live_slots[tile_index]
    selector = ((my_owner[None, :] == jnp.arange(tile_devices)[:, None]) & my_live[None, :]).astype(
        jnp.bfloat16
    )
    outgoing = jnp.dot(selector, encoded, preferred_element_type=jnp.float32).astype(jnp.bfloat16)
    incoming = lax.all_to_all(outgoing, "tile", split_axis=0, concat_axis=0, tiled=True)
    placement = jnp.any(
        (local_cell[None, :, :] == cell_ids[:, None, None]) & mine_mask[None, :, :], axis=2
    ).astype(jnp.bfloat16)
    block_cells = jnp.dot(placement, incoming, preferred_element_type=jnp.float32)
    grid_tokens = block_cells.astype(jnp.bfloat16).reshape(BLOCK, BLOCK, width_model)
    slide_in = layer_norm(block_cells, slide_gain, 1e-05).astype(jnp.bfloat16)
    slide_query = jnp.dot(slide_in, slide_full[0], preferred_element_type=jnp.float32).astype(
        jnp.bfloat16
    )
    slide_keys = jnp.dot(slide_in, slide_full[1], preferred_element_type=jnp.float32).astype(
        jnp.bfloat16
    )
    slide_values = jnp.dot(slide_in, slide_full[2], preferred_element_type=jnp.float32).astype(
        jnp.bfloat16
    )
    inner_width = slide_keys.shape[1]
    key_value_cells = jnp.concatenate([slide_keys, slide_values], axis=1).reshape(
        BLOCK, BLOCK, 2 * inner_width
    )
    surround = with_halo(key_value_cells, ((("tile", "row"), 0), ("col", 1)), BLOCK)
    near_rows = surround.reshape(-1, 2 * inner_width)
    near_keys = near_rows[:, :inner_width]
    near_values = near_rows[:, inner_width:]
    block_row = tile_index * row_devices + row_index
    padded = jnp.pad(occupancy, BLOCK)
    window = lax.dynamic_slice(
        padded, (block_row * BLOCK, column_index * BLOCK), (3 * BLOCK, 3 * BLOCK)
    )
    mask_row = block_mask.reshape(-1)
    mask_grid = jnp.concatenate([mask_row[:4], jnp.ones((1,), jnp.int32), mask_row[4:]]).reshape(
        3, 3
    )
    mask_cells = jnp.repeat(jnp.repeat(mask_grid, BLOCK, axis=0), BLOCK, axis=1)
    usable = (window * mask_cells).reshape(-1) > 0
    query_live = (
        lax.dynamic_slice(occupancy, (block_row * BLOCK, column_index * BLOCK), (BLOCK, BLOCK))
        .reshape(-1)
        .astype(jnp.float32)
    )
    head_count = inner_width // HDS
    scores = jnp.einsum(
        "qhd,khd->hqk",
        slide_query.reshape(-1, head_count, HDS),
        near_keys.reshape(-1, head_count, HDS),
        preferred_element_type=jnp.float32,
    ) / math.sqrt(HDS)
    allow = usable[None, None, :]
    row_peak = jnp.max(jnp.where(allow, scores, -1e30), axis=-1, keepdims=True)
    weights_exp = jnp.where(allow, jnp.exp(scores - row_peak), 0.0)
    live_query = query_live[None, :, None]
    soft = (
        weights_exp / (jnp.sum(weights_exp, axis=-1, keepdims=True) + 1.0 - live_query) * live_query
    ).astype(jnp.bfloat16)
    slide_mix = (
        jnp.einsum(
            "hqk,khd->qhd",
            soft,
            near_values.reshape(-1, head_count, HDS),
            preferred_element_type=jnp.float32,
        )
        .reshape(-1, inner_width)
        .astype(jnp.bfloat16)
    )
    slide_branch = contract_last(slide_mix, slide_full[3]).reshape(BLOCK, BLOCK, width_model)
    return (grid_tokens, slide_branch)


MESH_ID = pl.DeviceIdType.MESH
NEAR = [(-1, -1), (-1, 0), (-1, 1), (0, -1), (0, 1), (1, -1), (1, 0), (1, 1)]
FAR_BIAS = -1e30
PHASES = 8


def fits_fused(mesh):
    return (mesh.shape["tile"], mesh.shape["row"], mesh.shape["col"]) == (8, 2, 2)


def contract_rows(first_op, second_op):
    return lax.dot_general(
        first_op, second_op, (((1,), (1,)), ((), ())), preferred_element_type=jnp.float32
    )


def matmul(first_op, second_op):
    return jnp.dot(first_op, second_op, preferred_element_type=jnp.float32)


def fused_kernel(
    sizes,
    cell_ref,
    count_ref,
    mask_ref,
    tok_hbm,
    enc_gain_hbm,
    final_gain_hbm,
    slide_gain_hbm,
    wq_hbm,
    wk_hbm,
    wv_hbm,
    wo_hbm,
    wp_hbm,
    sq_hbm,
    sk_hbm,
    sv_hbm,
    so_hbm,
    grid_ref,
    branch_ref,
    cls,
    tok,
    normed,
    s1,
    r1,
    s2,
    r2,
    s3,
    r3,
    s4,
    r4,
    s7,
    r7,
    s9,
    r9,
    sg,
    rg,
    halo_out,
    halo,
    wide,
    gains,
    live,
    slide_w,
    wq_ref,
    wk_ref,
    wv_ref,
    wo_ref,
    wp_ref,
    enc_gain_ref,
    final_gain_ref,
    slide_gain_ref,
    in_sem,
    send_sem,
    recv_sem,
    w_send,
    w_recv,
    halo_send,
    halo_recv,
    v_send,
    v_recv,
):
    tiles, rows_n, cols_n, slots, patch, width, inner = sizes
    shard = width // tiles
    half = inner // 2
    heads = inner // HD
    third = inner // slots
    third_heads = heads // slots
    bf, f32 = jnp.bfloat16, jnp.float32
    me = lax.axis_index("tile")
    my_row = lax.axis_index("row")
    my_col = lax.axis_index("col")
    block_row = me * rows_n + my_row

    first_in = pltpu.make_async_copy(tok_hbm.at[:, pl.ds(0, 16), :], cls, in_sem.at[0])
    first_in.start()
    whole_in = pltpu.make_async_copy(tok_hbm, tok, in_sem.at[1])
    gain_ins = []
    for place, (source, landing) in enumerate(
        (
            (enc_gain_hbm, enc_gain_ref),
            (final_gain_hbm, final_gain_ref),
            (slide_gain_hbm, slide_gain_ref),
        )
    ):
        gain_ins.append(pltpu.make_async_copy(source, landing, in_sem.at[2 + place]))
        gain_ins[-1].start()
    weight_ins = []
    cut = shard // 2
    wv_own = wv_hbm.at[pl.ds(pl.multiple_of(my_row * cut, cut), cut), :]
    for place, (source, landing) in enumerate(
        ((wq_hbm, wq_ref), (wp_hbm, wp_ref), (wk_hbm, wk_ref), (wv_own, wv_ref.at[me, my_row]), (wo_hbm, wo_ref))
    ):
        weight_ins.append(pltpu.make_async_copy(source, landing, in_sem.at[5 + place]))
    wq_in, wp_in, wk_in, wv_in, wo_in = weight_ins
    wq_in.start()
    wv_in.start()
    mine = my_row * 2 + my_col
    own_pair = pl.ds(my_row * 2, 2)
    for which, source in enumerate((sq_hbm, sk_hbm, sv_hbm, so_hbm)):

        @pl.when(mine == which)
        def bring(source=source):
            pltpu.make_async_copy(source, slide_w.at[mine, me], in_sem.at[10]).start()

    own_in = pltpu.make_async_copy(sq_hbm, slide_w.at[mine, me], in_sem.at[10])
    wp_in.start()
    whole_in.start()
    for copy in (wk_in, wo_in):
        copy.start()

    blank = jnp.where(
        lax.broadcasted_iota(jnp.int32, (8, halo.shape[2]), 1) == halo_lane(halo), FAR_BIAS, 0.0
    )
    for place in range(9):
        halo[place] = blank

    barrier = pltpu.get_barrier_semaphore()
    for step in range(1, tiles):
        pl.semaphore_signal(
            barrier, inc=1, device_id={"tile": lax.rem(me + step, tiles)}, device_id_type=MESH_ID
        )
    beside = []
    near_count = jnp.int32(0)
    for down, right in NEAR:
        to_row = block_row + down
        to_col = my_col + right
        inside = (to_row >= 0) & (to_row < tiles * rows_n) & (to_col >= 0) & (to_col < cols_n)
        target = {
            "tile": lax.div(to_row + rows_n, rows_n) - 1,
            "row": lax.rem(to_row + rows_n, rows_n),
            "col": to_col,
        }
        beside.append((inside, target))
        near_count = near_count + inside.astype(jnp.int32)

        @pl.when(inside)
        def greet(target=target):
            pl.semaphore_signal(barrier, inc=1, device_id=target, device_id_type=MESH_ID)

    first_in.wait()
    raw = [cls[slot].astype(f32)[0:1] for slot in range(slots)]
    raw_rows = jnp.concatenate(raw, axis=0)
    for copy in gain_ins:
        copy.wait()
    enc_gain = enc_gain_ref[...].reshape(1, width)
    final_gain = final_gain_ref[...].reshape(1, width)
    class_normed = layer_norm(raw_rows, enc_gain, 1e-06).astype(bf).astype(f32)
    class_rows = jnp.concatenate(
        [class_normed] * 3 + [raw_rows, jnp.zeros((16 - 4 * slots, width), f32)], axis=0
    ).astype(bf)
    for to in range(tiles):
        s1[to, :, :shard] = class_rows[:, to * shard : (to + 1) * shard]
        gains[to, :, :shard] = jnp.broadcast_to(
            final_gain[:, to * shard : (to + 1) * shard], (8, shard)
        )

    pl.semaphore_wait(barrier, tiles - 1 + near_count)

    started = []

    def send(phase, source, landing):
        copies = []
        for step in range(1, tiles):
            to = lax.rem(me + step, tiles)
            copy = pltpu.make_async_remote_copy(
                src_ref=source.at[to] if len(source.shape) == len(landing.shape) else source,
                dst_ref=landing.at[me],
                send_sem=send_sem.at[phase, step],
                recv_sem=recv_sem.at[phase, step],
                device_id={"tile": to},
                device_id_type=MESH_ID,
            )
            copy.start()
            copies.append(copy)
        started.extend(copies)
        landing[me] = source[me] if len(source.shape) == len(landing.shape) else source[...]
        return copies

    def arrive(copies):
        for copy in copies:
            copy.wait_recv()

    copies1 = send(0, s1, r1)

    own_in.wait()

    def relay_copy(hop, side):
        onward = 2 if side == 0 else -2
        held = me - onward * hop
        return pltpu.make_async_remote_copy(
            src_ref=slide_w.at[mine, held],
            dst_ref=slide_w.at[mine, held],
            send_sem=w_send.at[side, hop],
            recv_sem=w_recv.at[side, hop],
            device_id={"tile": me + onward},
            device_id_type=MESH_ID,
        )

    def relay_inside(place):
        return (place >= 0) & (place < tiles)

    def relay_send(hop):
        for side, onward in ((0, 2), (1, -2)):

            @pl.when(relay_inside(me + onward) & relay_inside(me - onward * hop))
            def go(side=side):
                relay_copy(hop, side).start()

    def relay_sent(hop):
        for side, onward in ((0, 2), (1, -2)):

            @pl.when(relay_inside(me + onward) & relay_inside(me - onward * hop))
            def done(side=side):
                relay_copy(hop, side).wait_send()

    def relay_take(hop):
        for side, onward in ((0, 2), (1, -2)):
            held = me - onward * (hop + 1)

            @pl.when(relay_inside(held))
            def take(side=side, onward=onward, held=held):
                pltpu.make_async_remote_copy(
                    src_ref=slide_w.at[mine, held],
                    dst_ref=slide_w.at[mine, held],
                    send_sem=w_send.at[side, hop],
                    recv_sem=w_recv.at[side, hop],
                    device_id={"tile": me - onward},
                    device_id_type=MESH_ID,
                ).wait_recv()
                onward_slide(held)

    side_y = lax.rem(me, 2)

    def value_copy(target, held, way, hop):
        return pltpu.make_async_remote_copy(
            src_ref=wv_ref.at[held, my_row],
            dst_ref=wv_ref.at[held, my_row],
            send_sem=v_send.at[way, hop],
            recv_sem=v_recv.at[way, hop],
            device_id={"tile": target},
            device_id_type=MESH_ID,
        )

    def value_line(hop, method):
        for side, onward in ((0, 2), (1, -2)):

            @pl.when(relay_inside(me + onward) & relay_inside(me - onward * hop))
            def go(side=side, onward=onward):
                getattr(value_copy(me + onward, me - onward * hop, side, hop), method)()

    def value_take(hop):
        for side, onward in ((0, 2), (1, -2)):

            @pl.when(relay_inside(me - onward * (hop + 1)))
            def go(side=side, onward=onward):
                held = me - onward * (hop + 1)
                value_copy(me - onward, held, side, hop).wait_recv()
                value_across(held, side_y).start()

    def value_across(held, parity):
        place = lax.div(held, 2)
        return value_copy(me + 1 - 2 * side_y, place * 2 + parity, 2, place)

    def value_step(hop):
        value_take(hop)
        if hop < 2:
            value_line(hop + 1, "start")

    value_pair = pltpu.make_async_remote_copy(
        src_ref=wv_ref.at[:, my_row],
        dst_ref=wv_ref.at[:, my_row],
        send_sem=v_send.at[3, 0],
        recv_sem=v_recv.at[3, 0],
        device_id={"row": 1 - my_row},
        device_id_type=MESH_ID,
    )
    wv_in.wait()
    value_line(0, "start")
    value_across(me, side_y).start()
    lines = tiles // 2

    def across(place, parity):
        shard_at = place * 2 + parity
        return pltpu.make_async_remote_copy(
            src_ref=slide_w.at[mine, shard_at],
            dst_ref=slide_w.at[mine, shard_at],
            send_sem=w_send.at[2, place],
            recv_sem=w_recv.at[2, place],
            device_id={"tile": me + 1 - 2 * side_y},
            device_id_type=MESH_ID,
        )

    def over_x(shard_at, owned):
        return pltpu.make_async_remote_copy(
            src_ref=slide_w.at[owned, shard_at],
            dst_ref=slide_w.at[owned, shard_at],
            send_sem=w_send.at[3, shard_at],
            recv_sem=w_recv.at[3, shard_at],
            device_id={"col": 1 - my_col},
            device_id_type=MESH_ID,
        )

    def onward_slide(shard_at):
        across(lax.div(shard_at, 2), side_y).start()
        over_x(shard_at, mine).start()

    pair_copy = pltpu.make_async_remote_copy(
        src_ref=slide_w.at[own_pair],
        dst_ref=slide_w.at[own_pair],
        send_sem=w_send.at[4, 0],
        recv_sem=w_recv.at[4, 0],
        device_id={"row": 1 - my_row},
        device_id_type=MESH_ID,
    )
    relay_send(0)
    onward_slide(me)

    row64 = lax.broadcasted_iota(jnp.int32, (8 * tiles, 1), 0)
    in_block = lax.rem(row64, 8)

    def norm_chunk(chunk, carry):
        rows = pl.ds(pl.multiple_of(chunk * 32, 32), 32)
        inside = pl.ds(pl.multiple_of(lax.rem(chunk, per_tile) * 32, 32), 32)
        wide_rows_in = tok[lax.div(chunk, per_tile), inside, :].astype(f32)
        normed[rows, :] = layer_norm(wide_rows_in, enc_gain, 1e-06).astype(bf)
        return carry

    per_tile = patch // 32
    whole_chunks = slots * per_tile
    my_gain = gains[me][:, :shard]
    wp_in.wait()
    gain_high = my_gain.astype(bf)
    gain_low = (my_gain - gain_high.astype(f32)).astype(bf)
    sums = [
        matmul(gain_high, wp_ref[:, cut : cut + half])
        + matmul(gain_low, wp_ref[:, cut : cut + half])
        for cut in (0, half)
    ]
    low_rows = lax.broadcasted_iota(jnp.int32, (8, 1), 0) < 4
    sg[...] = jnp.where(low_rows, sums[0], sums[1])
    copies_g = send(7, sg, rg)

    arrive(copies1)
    wq_in.wait()
    shards1 = r1[...].reshape(16 * tiles, r1.shape[2])[:, :shard]
    in_wide = lax.rem(lax.broadcasted_iota(jnp.int32, (16 * tiles, 1), 0), 16)
    parts = [matmul(shards1, wq_ref[:, third * k : third * (k + 1)]) for k in range(3)]
    packed_part = jnp.where(
        in_wide < slots, parts[0], jnp.where(in_wide < 2 * slots, parts[1], parts[2])
    )
    s2[...] = packed_part.astype(bf).reshape(s2.shape)
    copies2 = send(1, s2, r2)
    value_step(0)
    relay_take(0)
    relay_send(1)
    whole_in.wait()
    lax.fori_loop(0, whole_chunks // 3, norm_chunk, 0)
    arrive(copies2)
    s3[...] = jnp.sum(r2[...].astype(f32), axis=0).astype(bf)
    copies3 = send(2, s3, r3)
    value_step(1)
    relay_take(1)
    relay_send(2)
    lax.fori_loop(whole_chunks // 3, 2 * (whole_chunks // 3), norm_chunk, 0)

    wide_rows = 48 * tiles
    exp_row = lax.broadcasted_iota(jnp.int32, (wide_rows, 16 * tiles), 0)
    exp_col = lax.broadcasted_iota(jnp.int32, (wide_rows, 16 * tiles), 1)
    exp_in = lax.rem(exp_row, 48)
    exp_slot = lax.div(exp_in, heads)
    exp_head = lax.rem(exp_in, heads)
    exp_turn = lax.div(exp_head, third_heads)
    exp_base = lax.div(exp_row, 48) * 16 + exp_turn * slots + exp_slot
    pick = ((exp_slot < slots) & (exp_col == exp_base)).astype(f32).astype(bf)
    head_of_row = lax.rem(
        lax.rem(lax.broadcasted_iota(jnp.int32, (wide_rows, third), 0), 48), heads
    )
    head_of_col = lax.div(lax.broadcasted_iota(jnp.int32, (wide_rows, third), 1), HD)
    own = [head_of_row == head_of_col + turn * third_heads for turn in range(3)]
    arrive(copies3)
    wk_in.wait()
    queries = matmul(pick, r3[...].reshape(16 * tiles, third))
    query_wide = jnp.concatenate([jnp.where(at, queries, 0.0) for at in own], axis=1).astype(bf)
    folded = contract_rows(query_wide, wk_ref[...])
    s4[:, :, :shard] = folded.astype(bf).reshape(tiles, 48, shard)
    copies4 = send(3, s4, r4)
    value_step(2)
    relay_take(2)
    lax.fori_loop(2 * (whole_chunks // 3), whole_chunks, norm_chunk, 0)
    arrive(copies4)
    for place in range(lines):
        value_across(jnp.int32(2 * place), 1 - side_y).wait_recv()
    value_pair.start()
    for place in range(lines):
        across(place, 1 - side_y).wait_recv()
        over_x(place * 2 + 1 - side_y, mine).start()

    for other in range(tiles):
        wide[:, other * shard : (other + 1) * shard] = r4[other, :, :shard]
    tokens = normed[...]
    scores = contract_rows(wide[...], tokens) / math.sqrt(HD)
    score_slot = lax.div(lax.broadcasted_iota(jnp.int32, scores.shape, 0), heads)
    score_tile = lax.div(lax.broadcasted_iota(jnp.int32, scores.shape, 1), patch)
    same = score_slot == score_tile
    peak = jnp.max(jnp.where(same, scores, -1e30), axis=1, keepdims=True)
    grown = jnp.where(same, jnp.exp(jnp.minimum(scores - peak, 0.0)), 0.0)
    total = jnp.sum(grown, axis=1, keepdims=True)
    probs = (grown / jnp.where(total > 0.0, total, 1.0)).astype(bf)
    mixed = matmul(probs, tokens).astype(bf)
    value_pair.wait_recv()
    all_values = matmul(mixed, wv_ref[...].reshape(width, inner))
    valued = jnp.zeros((48, third), f32)
    for turn in range(3):
        columns = all_values[:, third * turn : third * (turn + 1)]
        valued = jnp.where(own[turn][:48], columns, valued)
    s7[...] = lax.dot_general(
        pick[:48, :16], valued.astype(bf), (((0,), (0,)), ((), ())), preferred_element_type=f32
    ).astype(bf)
    copies7 = send(6, s7, r7)
    col64 = lax.broadcasted_iota(jnp.int32, (8 * tiles, 16 * tiles), 1)
    row_full = lax.broadcasted_iota(jnp.int32, (8 * tiles, 16 * tiles), 0)
    place_low = jnp.zeros((8 * tiles, 16 * tiles), f32)
    grid_cols = BLOCK * cols_n
    group = my_row * cols_n + my_col
    row_key = lax.div(row_full, 8) * 4 + lax.rem(row_full, 4)
    for other in range(tiles):
        device = other * rows_n * cols_n + group
        count = count_ref[device]
        for slot in range(slots):
            cell = cell_ref[device * slots + slot]
            cell_row = lax.div(cell, jnp.int32(grid_cols))
            cell_col = lax.rem(cell, jnp.int32(grid_cols))
            owner = lax.div(cell_row, jnp.int32(BLOCK * rows_n))
            spot = owner * 4 + lax.rem(cell_row, BLOCK) * BLOCK + lax.rem(cell_col, BLOCK)
            spot = jnp.where(slot < count, spot, -1)
            hit = (row_key == spot) & (col64 == other * 16 + slot)
            place_low = jnp.where(hit, 1.0, place_low)
    placing = [
        jnp.concatenate(
            [jnp.zeros((8 * tiles, slots * turn), f32), place_low[:, : -slots * turn]], axis=1
        ).astype(bf)
        for turn in range(1, 4)
    ]
    live_col = jnp.sum(place_low, axis=1, keepdims=True)
    live[...] = jnp.broadcast_to(live_col, (8 * tiles, 128)).reshape(tiles, 8, 128)
    placing.insert(0, place_low.astype(bf))
    raw_cells = matmul(placing[3], shards1)

    arrive(copies7)
    wo_in.wait()

    mix_rows = r7[...].reshape(16 * tiles, third)
    cell_mix = jnp.concatenate([matmul(placing[k], mix_rows) for k in range(3)], axis=1)
    carried = raw_cells + contract_rows(cell_mix.astype(bf), wo_ref[...])
    part_mean = jnp.mean(carried, axis=1, keepdims=True)
    centered = carried - part_mean
    part_square = jnp.sum(centered * centered, axis=1, keepdims=True)
    scaled = (centered * my_gain[0:1]).astype(bf)
    landed = jnp.where(
        in_block < 4, matmul(scaled, wp_ref[:, :half]), matmul(scaled, wp_ref[:, half:])
    )
    s9[:, :, :half] = landed.reshape(tiles, 8, half)
    lane = lax.broadcasted_iota(jnp.int32, (8 * tiles, 128), 1)
    s9[:, :, half:] = jnp.where(lane == 0, part_mean, part_square).reshape(tiles, 8, 128)
    copies9 = send(8, s9, r9)
    for shard_at in range(tiles):
        over_x(shard_at, my_row * 2 + 1 - my_col).wait_recv()
    pair_copy.start()
    arrive(copies_g)
    arrive(copies9)

    means = [r9[other, :, half : half + 1] for other in range(tiles)]
    mean = sum(means) / tiles
    square = sum(
        r9[other, :, half + 1 : half + 2] + shard * (means[other] - mean) ** 2
        for other in range(tiles)
    )
    joined = sum(
        r9[other, :, :half] + (means[other] - mean) * rg[other] for other in range(tiles)
    )
    joined = (joined * lax.rsqrt(square / width + 1e-06)).astype(bf)
    cells32 = joined.astype(f32)
    cells = jnp.concatenate([cells32[0:4], cells32[4:8]], axis=1)
    grid_ref[0] = cells[0:2].astype(bf)
    grid_ref[1] = cells[2:4].astype(bf)

    pair_copy.wait_recv()
    inner_s = slide_w.shape[3]
    slide_rows = jnp.concatenate([cells, cells], axis=0)
    slide_in = layer_norm(slide_rows, slide_gain_ref[...].reshape(1, -1), 1e-05).astype(bf)

    def slide_full(which):
        return slide_w[which].reshape(-1, inner_s)

    keys = matmul(slide_in, slide_full(1))
    values = matmul(slide_in, slide_full(2))
    my_live = live[me][:, 0:1]
    halo_out[:, :inner_s] = jnp.where(low_rows, keys, values).astype(bf).astype(f32)
    lane8 = lax.broadcasted_iota(jnp.int32, (8, 128), 1)
    halo_out[:, inner_s:] = jnp.where(
        (lane8 == 0) & jnp.logical_not(low_rows & (my_live > 0.0)), FAR_BIAS, 0.0
    )
    places = [0, 1, 2, 3, 5, 6, 7, 8]
    halo_copies = []
    for index, (inside, target) in enumerate(beside):
        copy = pltpu.make_async_remote_copy(
            src_ref=halo_out,
            dst_ref=halo.at[8 - places[index]],
            send_sem=halo_send.at[index],
            recv_sem=halo_recv.at[7 - index],
            device_id=target,
            device_id_type=MESH_ID,
        )

        @pl.when(inside)
        def send_halo(copy=copy):
            copy.start()

        halo_copies.append(copy)
    halo[4] = halo_out[...]
    slide_query = matmul(slide_in, slide_full(0)).astype(bf).astype(f32)
    slide_heads = inner_s // HDS
    head_lane = lax.div(lax.broadcasted_iota(jnp.int32, (8, inner_s), 1), HDS)
    one_lane = jnp.where(lane8 == 0, math.sqrt(HDS), 0.0)
    query_heads = jnp.concatenate(
        [
            jnp.concatenate([jnp.where(head_lane == head, slide_query, 0.0), one_lane], axis=1)
            for head in range(slide_heads)
        ],
        axis=0,
    ).astype(bf)
    for index, (inside, target) in enumerate(beside):
        arriving = pltpu.make_async_remote_copy(
            src_ref=halo_out,
            dst_ref=halo.at[places[index]],
            send_sem=halo_send.at[index],
            recv_sem=halo_recv.at[index],
            device_id=target,
            device_id_type=MESH_ID,
        )

        @pl.when(inside)
        def take_halo(arriving=arriving):
            arriving.wait_recv()

    lane_wide = lax.broadcasted_iota(jnp.int32, (8, halo.shape[2]), 1)
    near = []
    for place in range(9):
        rows = halo[place]
        if place != 4:
            shut = mask_ref[0, 0, places.index(place)] == 0
            rows = jnp.where((lane_wide == inner_s) & shut, FAR_BIAS, rows)
        near.append(rows)
    near = jnp.concatenate(near, axis=0)
    near_keys = near.astype(bf)
    near_values = jnp.concatenate([near[4:], near[:4]], axis=0)[:, :inner_s].astype(bf)
    slide_scores = contract_rows(query_heads, near_keys) / math.sqrt(HDS)
    slide_peak = jnp.max(slide_scores, axis=1, keepdims=True)
    slide_exp = jnp.exp(slide_scores - slide_peak)
    alive = jnp.concatenate([my_live] * slide_heads, axis=0)
    soft = (
        slide_exp / (jnp.sum(slide_exp, axis=1, keepdims=True) + 1.0 - alive) * alive
    ).astype(bf)
    mix_heads = matmul(soft, near_values)
    slide_mix = sum(
        jnp.where(head_lane == head, mix_heads[8 * head : 8 * head + 8], 0.0)
        for head in range(slide_heads)
    ).astype(bf)
    branch = contract_rows(slide_mix, slide_full(3))
    branch_ref[0] = branch[0:2]
    branch_ref[1] = branch[2:4]

    for copy in started + [across(place, side_y) for place in range(lines)] + [pair_copy]:
        copy.wait_send()
    value_pair.wait_send()
    for shard_at in range(tiles):
        over_x(shard_at, mine).wait_send()
    for place in range(lines):
        value_across(jnp.int32(2 * place), side_y).wait_send()
    for hop in range(3):
        relay_sent(hop)
        value_line(hop, "wait_send")
    for (inside, target), copy in zip(beside, halo_copies):

        @pl.when(inside)
        def sent_halo(copy=copy):
            copy.wait_send()


def halo_lane(halo):
    return halo.shape[2] - 128


def fused(
    tile_tokens,
    tile_count,
    tile_cell,
    occupancy,
    block_mask,
    enc_gain,
    w_query,
    w_key,
    w_value,
    w_out_t,
    final_gain,
    w_proj,
    slide_gain,
    s_query,
    s_key,
    s_value,
    s_out_t,
):
    tiles = lax.axis_size("tile")
    rows_n = lax.axis_size("row")
    cols_n = lax.axis_size("col")
    slots, patch, width = tile_tokens.shape
    inner = w_query.shape[1]
    model = w_proj.shape[1]
    inner_s = s_query.shape[1]
    half = inner // 2
    sizes = (tiles, rows_n, cols_n, slots, patch, width, inner)
    bf, f32 = jnp.bfloat16, jnp.float32
    vmem = pl.BlockSpec(memory_space=pltpu.VMEM)
    smem = pl.BlockSpec(memory_space=pltpu.SMEM)
    slab = pltpu.VMEM((tiles, 16, 256), bf)
    thirds = pltpu.VMEM((tiles, 16, inner // 3), bf)
    one_third = pltpu.VMEM((16, inner // 3), bf)
    packed = pltpu.VMEM((tiles, 8, half), f32)
    one_packed = pltpu.VMEM((8, half), f32)
    heads_slab = pltpu.VMEM((tiles, 48, 256), bf)
    stat_slab = pltpu.VMEM((tiles, 8, half + 128), f32)

    def kernel(*refs):
        fused_kernel(sizes, *refs)

    return pl.pallas_call(
        kernel,
        out_shape=(
            jax.ShapeDtypeStruct((BLOCK, BLOCK, model), bf),
            jax.ShapeDtypeStruct((BLOCK, BLOCK, model), f32),
        ),
        in_specs=[smem] * 3 + [pl.BlockSpec(memory_space=pl.ANY)] * 13,
        out_specs=(vmem, vmem),
        scratch_shapes=[
            pltpu.VMEM((slots, 16, width), bf),
            pltpu.VMEM((slots, patch, width), bf),
            pltpu.VMEM((slots * patch, width), bf),
            slab,
            slab,
            thirds,
            thirds,
            one_third,
            thirds,
            heads_slab,
            heads_slab,
            one_third,
            thirds,
            stat_slab,
            stat_slab,
            one_packed,
            packed,
            pltpu.VMEM((8, inner_s + 128), f32),
            pltpu.VMEM((9, 8, inner_s + 128), f32),
            pltpu.VMEM((48, width), bf),
            pltpu.VMEM((tiles, 8, 256), f32),
            pltpu.VMEM((tiles, 8, 128), f32),
            pltpu.VMEM((4, tiles, s_query.shape[0], inner_s), bf),
            pltpu.VMEM(w_query.shape, bf),
            pltpu.VMEM(w_key.shape, bf),
            pltpu.VMEM((tiles, 2, w_value.shape[0] // 2, inner), bf),
            pltpu.VMEM(w_out_t.shape, bf),
            pltpu.VMEM(w_proj.shape, bf),
            pltpu.VMEM((width,), f32),
            pltpu.VMEM((width,), f32),
            pltpu.VMEM((model,), f32),
            pltpu.SemaphoreType.DMA((12,)),
            pltpu.SemaphoreType.DMA((PHASES + 1, tiles)),
            pltpu.SemaphoreType.DMA((PHASES + 1, tiles)),
            pltpu.SemaphoreType.DMA((5, tiles)),
            pltpu.SemaphoreType.DMA((5, tiles)),
            pltpu.SemaphoreType.DMA((8,)),
            pltpu.SemaphoreType.DMA((8,)),
            pltpu.SemaphoreType.DMA((4, 4)),
            pltpu.SemaphoreType.DMA((4, 4)),
        ],
        compiler_params=pltpu.CompilerParams(
            collective_id=0, has_side_effects=True, vmem_limit_bytes=60 * 1024 * 1024
        ),
    )(
        tile_cell,
        tile_count,
        block_mask,
        tile_tokens,
        enc_gain,
        final_gain,
        slide_gain,
        w_query,
        w_key,
        w_value,
        w_out_t,
        w_proj,
        s_query,
        s_key,
        s_value,
        s_out_t,
    )


def solution(mesh):
    placed = (
        P(("tile", "row", "col"), None, None),
        P(),
        P(),
        P(),
        P(("tile", "row"), "col", None),
        P(),
        P("tile", None),
        P("tile", None),
        P("tile", None),
        P("tile", None),
        P(),
        P("tile", None),
        P(),
        P("tile", None),
        P("tile", None),
        P("tile", None),
        P("tile", None),
    )
    per_device = fused if fits_fused(mesh) else local
    return jax.shard_map(
        per_device,
        mesh=mesh,
        in_specs=placed,
        out_specs=(P(("tile", "row"), "col", None), P(("tile", "row"), "col", None)),
        check_vma=False,
    )
```
